32 devices in a mesh: grp: 4 (over y, core), sub: 8 (over z, x).
Axes of the slice: x: 2, y: 2, z: 4, core: 2. Of those that a mesh axis runs over, the one named last changes fastest.
Arguments:
- cluster_pos: float32 [3, 1024], P(None, 'sub'), may hold values from -3 to 3
- cluster_vel: float32 [3, 1024], P(None, 'sub'), may hold values from -15 to 15
- cluster_mass: float32 [1024], P('sub'), may hold values from 3 to 60
- galaxy_pos: float32 [3, 16384], P(None, ('grp', 'sub')), may hold values from -1 to 7
- galaxy_vel: float32 [3, 16384], P(None, ('grp', 'sub')), may hold values from -3 to 3
- galaxy_kind: int32 [16384], P(('grp', 'sub')), may hold values from 0 to 3
- species_mass: float32 [4], replicated, may hold values from 10 to 80
Outputs:
- cluster_pos_out: float32 [3, 1024], P(None, 'sub')
- cluster_vel_out: float32 [3, 1024], P(None, 'sub')
- galaxy_pos_out: float32 [3, 16384], P(None, ('grp', 'sub'))
- galaxy_vel_out: float32 [3, 16384], P(None, ('grp', 'sub'))
The draws below stay inside these ranges and needn't reach their ends.
All inputs are finite; a program needn't handle non-finite values.
Results may differ from the reference program's by a relative error of at most 0.0003.
Values sent between devices are 32-bit elements; how exact they have to be, the bound alone decides.
No kernel may reach another device: no remote copies, remote signals or barrier semaphores. Data moves between devices by JAX's collectives and lax.ppermute only.
A program may use at most 64 MiB of HBM per device.

```python
import math
import jax
import jax.numpy as jnp
import numpy as np
from jax import lax

G_DEV = 512
SUBSTEPS = 8
KINDS = 4
NC = 1024
NG = 16384


def place_ends(values, own_key, low, high):
    shape = values.shape
    spot = [jax.random.randint(jax.random.fold_in(own_key, axis), (), 0, shape[axis]) for axis in range(len(shape))]
    values = values.at[tuple(spot)].set(low)
    longest = shape.index(max(shape))
    spot[longest] = (spot[longest] + 1) % shape[longest]
    return values.at[tuple(spot)].set(high)


def level_of(key, extent, cuts, least, top_value):
    factor_of = 1.0
    for dim, parts in cuts:
        draws = jax.random.uniform(jax.random.fold_in(jax.random.fold_in(key, 6), dim), (parts,), jnp.float32, least / len(cuts), top_value / len(cuts))
        factor_of = factor_of * jnp.repeat(jnp.exp(draws), extent[dim] // parts).reshape((-1,) + (1,) * (len(extent) - 1 - dim))
    return factor_of


def rank_table(number_of, lean):
    loads = [(1 << 20) // math.isqrt(rank ** lean) + 1 for rank in range(1, number_of + 1)]
    spread = 1 + sum(loads) // (1 << 30)
    return np.cumsum(np.array([max(1, weight // spread) for weight in loads]))


def ranked(stream_key, extent, count, lean):
    listing = rank_table(count, lean)
    ticket = jax.random.randint(jax.random.fold_in(stream_key, 1), extent, 0, int(listing[count - 1]))
    grade = jnp.searchsorted(jnp.asarray(listing, jnp.int32), ticket, side="right")
    return jax.random.permutation(jax.random.fold_in(stream_key, 2), count)[grade].astype(jnp.int32)


def normal_values(key, extent, width, limit, split=(), held_as=jnp.bfloat16):
    drawn = jax.random.normal(key, extent, jnp.float32) * width
    if len(split) > 0:
        drawn = level_of(key, extent, split, -0.22, 0.18) * drawn
    return jnp.clip(drawn, min=-limit, max=limit).astype(held_as)


def setup_inputs(seed: int = 0) -> dict:
    key_of = jax.random.split(jax.random.key(seed), 8)
    return {
        "cluster_pos": normal_values(key_of[0], (3, NC), 0.5, 3.0, ((1, 8),), jnp.float32),
        "cluster_vel": normal_values(key_of[1], (3, NC), 2.5, 15.0, ((1, 8),), jnp.float32),
        "cluster_mass": jnp.clip(jnp.exp(math.log(60.0) - 2.9957323 * jax.random.uniform(key_of[2], (NC,), jnp.float32) ** level_of(key_of[2], (NC,), ((0, 8),), -0.2, 0.2)), 3.0, 60.0),
        "galaxy_pos": jnp.clip(-1.0 + 8.0 * jax.random.uniform(key_of[3], (3, NG), jnp.float32) ** level_of(key_of[3], (3, NG), ((1, 32),), -0.2, 0.2), -1.0, 7.0),
        "galaxy_vel": normal_values(key_of[4], (3, NG), 0.5, 3.0, ((1, 32),), jnp.float32),
        "galaxy_kind": place_ends(ranked(key_of[5], (NG,), KINDS, 2), jax.random.fold_in(key_of[5], 3), 0, KINDS - 1).astype(jnp.int32),
        "species_mass": jnp.clip(jnp.exp(jax.random.uniform(key_of[6], (KINDS,), jnp.float32, math.log(10.0), math.log(80.0))), 10.0, 80.0),
    }


step_time = 0.5
bridge_soft = 0.01
cluster_soft = 0.0025
tile_limit = 524288

def pick_block(target_count, source_count):
    tile_size = target_count
    while tile_size > 1 and (tile_size * source_count > tile_limit or target_count % tile_size != 0):
        tile_size = tile_size // 2
    return tile_size

def field(targets, sources, masses, soften):
    target_count = targets.shape[1]
    tile_size = pick_block(target_count, sources.shape[1])

    def one_tile(target_tile):
        separation = sources[:, None, :] - target_tile[:, :, None]
        distance = lax.optimization_barrier(jnp.sum(separation * separation, axis=0)) + soften
        inverse = lax.rsqrt(distance)
        weight = masses[None, :] * inverse * inverse * inverse
        return lax.optimization_barrier(jnp.sum(separation * weight[None], axis=2))
    stacked = targets.reshape(3, target_count // tile_size, tile_size).transpose(1, 0, 2)
    result = lax.map(one_tile, stacked)
    return result.transpose(1, 0, 2).reshape(3, target_count)

def rates(target_pos, target_vel, source_pos, source_vel, masses, soften):
    target_count = target_pos.shape[1]
    tile_size = pick_block(target_count, source_pos.shape[1])

    def one_tile(target_tile):
        separation = source_pos[:, None, :] - target_tile[:3, :, None]
        closing = source_vel[:, None, :] - target_tile[3:, :, None]
        distance = lax.optimization_barrier(jnp.sum(separation * separation, axis=0)) + soften
        inverse = lax.rsqrt(distance)
        weight = masses[None, :] * inverse * inverse * inverse
        radial = 3.0 * lax.optimization_barrier(jnp.sum(separation * closing, axis=0)) / distance
        acceleration = lax.optimization_barrier(jnp.sum(separation * weight[None], axis=2))
        jerk_rate = lax.optimization_barrier(jnp.sum((closing - radial[None] * separation) * weight[None], axis=2))
        return jnp.concatenate([acceleration, jerk_rate], axis=0)
    stacked = jnp.concatenate([target_pos, target_vel], axis=0)
    stacked = stacked.reshape(6, target_count // tile_size, tile_size).transpose(1, 0, 2)
    result = lax.map(one_tile, stacked)
    return result.transpose(1, 0, 2).reshape(6, target_count)

def galaxy_pull(targets, galaxy_positions, body_mass):
    blocks = NG // G_DEV
    block_pos = galaxy_positions.reshape(3, blocks, G_DEV).transpose(1, 0, 2)
    block_mass = body_mass.reshape(blocks, G_DEV)

    def add_block(running, item):
        return (running + field(targets, item[0], item[1], bridge_soft), None)
    running, unused = lax.scan(add_block, jnp.zeros((3, targets.shape[1]), jnp.float32), (block_pos, block_mass))
    return running

def reference(cluster_pos, cluster_vel, cluster_mass, galaxy_pos, galaxy_vel, galaxy_kind, species_mass):
    star_mass = cluster_mass / NC
    species = jnp.arange(KINDS, dtype=jnp.int32)
    body_mass = lax.optimization_barrier(jnp.sum(jnp.where(galaxy_kind[None, :] == species[:, None], species_mass[:, None], 0.0), axis=0)) / NG
    half_step = step_time / 2.0
    star_vel = cluster_vel + half_step * galaxy_pull(cluster_pos, galaxy_pos, body_mass)
    body_vel = galaxy_vel + half_step * field(galaxy_pos, cluster_pos, star_mass, bridge_soft)
    body_pos = galaxy_pos + step_time * body_vel
    substep_time = step_time / SUBSTEPS
    positions, velocity = (cluster_pos, star_vel)
    both = rates(positions, velocity, positions, velocity, star_mass, cluster_soft)
    acceleration, jerk_rate = (both[:3], both[3:])
    for substep in range(SUBSTEPS):
        guess_pos = positions + substep_time * (velocity + substep_time * (acceleration / 2.0 + substep_time * jerk_rate / 6.0))
        guess_vel = velocity + substep_time * (acceleration + substep_time * jerk_rate / 2.0)
        fresh = rates(guess_pos, guess_vel, guess_pos, guess_vel, star_mass, cluster_soft)
        new_acc, new_jerk = (fresh[:3], fresh[3:])
        new_vel = velocity + substep_time / 2.0 * (acceleration + new_acc) + substep_time * substep_time / 12.0 * (jerk_rate - new_jerk)
        new_pos = positions + substep_time / 2.0 * (velocity + new_vel) + substep_time * substep_time / 12.0 * (acceleration - new_acc)
        positions, velocity, acceleration, jerk_rate = (new_pos, new_vel, new_acc, new_jerk)
    final_vel = velocity + half_step * galaxy_pull(positions, body_pos, body_mass)
    final_body_vel = body_vel + half_step * field(body_pos, positions, star_mass, bridge_soft)
    return (positions, final_vel, body_pos, final_body_vel)
```

```python
import functools

import jax
import jax.numpy as jnp
from jax import lax
from jax.experimental import pallas as pl
from jax.experimental.pallas import tpu as pltpu
from jax.sharding import PartitionSpec as P

SUBSTEPS = 8

step_time = 0.5
bridge_soft = 0.01
cluster_soft = 0.0025
f32 = jnp.float32
bf16 = jnp.bfloat16
vmem_limit = 48 * 1024 * 1024


def parts(x, count):
    terms = []
    for _ in range(count):
        term = x.astype(bf16).astype(f32)
        terms.append(term)
        x = x - term
    return terms


def rows(pieces, total):
    have = sum(piece.shape[0] for piece in pieces)
    if have < total:
        pieces = pieces + [jnp.zeros((total - have, pieces[0].shape[1]), f32)]
    return jnp.concatenate(pieces, axis=0)


def dot(a, b):
    return lax.dot_general(a, b, (((1,), (0,)), ((), ())), preferred_element_type=f32)


def dot_t(a, b):
    return lax.dot_general(a, b, (((1,), (1,)), ((), ())), preferred_element_type=f32)


def square(x):
    return jnp.sum(x * x, axis=0, keepdims=True)


def distance_from(pos, scale, soften):
    a = parts(-2.0 * scale * pos, 3)
    s = parts(scale, 3)
    e = parts(scale * (square(pos) + soften), 3)
    return rows(
        [a[0], a[0], a[0], a[1], a[1], a[2], s[0], s[0], s[0], s[1], s[1], s[2], *e], 32
    )


def distance_to(pos):
    p = parts(pos, 3)
    q = parts(square(pos), 3)
    one = jnp.ones_like(q[0])
    return rows(
        [p[0], p[1], p[2], p[0], p[1], p[0], q[0], q[1], q[2], q[0], q[1], q[0], one, one, one], 32
    )


def closing_from(pos, vel, scale):
    b = parts(-3.0 * scale * pos, 2)
    w = parts(-3.0 * scale * vel, 2)
    k = parts(3.0 * scale, 2)
    d = parts(3.0 * scale * jnp.sum(pos * vel, axis=0, keepdims=True), 2)
    return rows([b[0], b[0], b[1], w[0], w[0], w[1], k[0], k[0], k[1], *d], 32)


def closing_to(pos, vel):
    p = parts(pos, 2)
    v = parts(vel, 2)
    c = parts(jnp.sum(pos * vel, axis=0, keepdims=True), 2)
    one = jnp.ones_like(c[0])
    return rows([v[0], v[1], v[0], p[0], p[1], p[0], c[0], c[1], c[0], one, one], 32)


def split_rows(pos):
    return parts(pos, 3) + [jnp.ones_like(pos[:1])]


def moment(total, pos):
    return total[0:3] + total[3:6] + total[6:9] - pos * total[9:10]


def block_of(count, most):
    size = most
    while count % size:
        size //= 2
    return size


def evaluate(pos, vel, scale, from_ref, to_ref, sum_ref, out_ref):
    n = pos.shape[1]
    fill = jnp.concatenate(
        [distance_from(pos, scale, cluster_soft), closing_from(pos, vel, scale)], axis=0
    )
    from_ref[...] = fill.T.astype(bf16)
    to_ref[0:32, :] = distance_to(pos).astype(bf16)
    to_ref[32:64, :] = closing_to(pos, vel).astype(bf16)
    sum_ref[...] = jnp.concatenate(split_rows(pos) + parts(vel, 2), axis=0).astype(bf16)
    ti = block_of(n, 1024)
    tj = block_of(n, 256)

    def one_block(j, carry):
        lanes = pl.ds(j, tj)
        weight_sum = jnp.zeros((16, tj), f32)
        radial_sum = jnp.zeros((16, tj), f32)
        for i in range(0, n, ti):
            across = slice(i, i + ti)
            distance = dot(from_ref[across, 0:32], to_ref[0:32, lanes])
            closing = dot(from_ref[across, 32:64], to_ref[32:64, lanes])
            inverse = lax.rsqrt(distance)
            square_inverse = inverse * inverse
            weight = square_inverse * inverse
            radial = weight * square_inverse * closing
            high = weight.astype(bf16)
            low = (weight - high.astype(f32)).astype(bf16)
            radial_high = radial.astype(bf16)
            radial_low = (radial - radial_high.astype(f32)).astype(bf16)
            source = sum_ref[:, across]
            weight_sum += dot(source, high) + dot(source, low)
            radial_sum += dot(source, radial_high) + dot(source, radial_low)
        out_ref[0:16, lanes] = weight_sum
        out_ref[16:32, lanes] = radial_sum
        return carry

    if n // tj <= 4:
        for j in range(0, n, tj):
            one_block(j, 0)
    else:
        lax.fori_loop(0, n // tj, lambda k, c: one_block(pl.multiple_of(k * tj, tj), c), 0)
    total = out_ref[...]
    acceleration = moment(total, pos)
    jerk_rate = total[10:13] + total[13:16] - vel * total[9:10] - moment(total[16:32], pos)
    return acceleration, jerk_rate


def add_up(refs):
    values = [ref[...] for ref in refs]
    while len(values) > 1:
        values = [a + b for a, b in zip(values[::2], values[1::2])]
    return values[0]


def hermite_kernel(pull_count, stars_ref, *refs):
    pulls, (stars_out, pos_out, vel_out, from_ref, to_ref, sum_ref, out_ref) = (
        refs[:pull_count],
        refs[pull_count:],
    )
    own = pos_out.shape[1]
    pos = stars_ref[0:3, :]
    vel = stars_ref[3:6, :] + (step_time / 2.0) * add_up(pulls)
    scale = stars_ref[7:8, :]
    middle = jnp.mean(pos, axis=1, keepdims=True)
    drift = jnp.mean(vel, axis=1, keepdims=True)
    h = step_time / SUBSTEPS

    def rates(x, v):
        return evaluate(x, v, scale, from_ref, to_ref, sum_ref, out_ref)

    pos = pos - middle
    vel = vel - drift
    acc, jerk = rates(pos, vel)

    def substep(_, carry):
        pos, vel, acc, jerk = carry
        guess_pos = pos + h * (vel + h * (acc * 0.5 + (h / 6.0) * jerk))
        guess_vel = vel + h * (acc + (h / 2.0) * jerk)
        new_acc, new_jerk = rates(guess_pos, guess_vel)
        new_vel = vel + (h / 2.0) * (acc + new_acc) + (h * h / 12.0) * (jerk - new_jerk)
        new_pos = pos + (h / 2.0) * (vel + new_vel) + (h * h / 12.0) * (acc - new_acc)
        return new_pos, new_vel, new_acc, new_jerk

    pos, vel, _, _ = lax.fori_loop(0, SUBSTEPS, substep, (pos, vel, acc, jerk))
    pos = pos + (middle + step_time * drift)
    vel = vel + drift
    stars_out[...] = jnp.concatenate([pos, vel, stars_ref[6:8, :]], axis=0)
    pos_out[...] = pos[:, :own]
    vel_out[...] = vel[:, :own]


def hermite(stars, pulls, own):
    n = stars.shape[1]
    pairs = n * n * (SUBSTEPS + 1)
    return pl.pallas_call(
        functools.partial(hermite_kernel, len(pulls)),
        out_shape=[
            jax.ShapeDtypeStruct(stars.shape, f32),
            jax.ShapeDtypeStruct((3, own), f32),
            jax.ShapeDtypeStruct((3, own), f32),
        ],
        scratch_shapes=[
            pltpu.VMEM((n, 64), bf16),
            pltpu.VMEM((64, n), bf16),
            pltpu.VMEM((16, n), bf16),
            pltpu.VMEM((32, n), f32),
        ],
        compiler_params=pltpu.CompilerParams(vmem_limit_bytes=vmem_limit),
        cost_estimate=pl.CostEstimate(flops=80 * pairs, bytes_accessed=0, transcendentals=pairs),
    )(stars, *pulls)


def center_of(stars, bodies):
    return 0.5 * (
        jnp.mean(stars, axis=1, keepdims=True) + jnp.mean(bodies, axis=1, keepdims=True)
    )


def weights(from_rows, to_columns):
    inverse = lax.rsqrt(dot(from_rows, to_columns))
    return inverse * inverse * inverse


def dot_high(sums, weight):
    return dot(sums, weight.astype(bf16))


def dot_both(sums, weight):
    high = weight.astype(bf16)
    return dot(sums, high) + dot(sums, (weight - high.astype(f32)).astype(bf16))


def kick_kernel(star_own, piece_count, *refs):
    pieces, (stars_out, bodies_out, pull_out, pos_out, vel_out, from_ref, sum_ref, pull_ref) = (
        refs[:piece_count],
        refs[piece_count:],
    )
    body_own = pos_out.shape[1]
    slot = 0
    for piece in pieces:
        for k in range(piece.shape[0]):
            stars_out[:, slot * star_own : (slot + 1) * star_own] = piece[k, :, :star_own]
            bodies_out[:, slot * body_own : (slot + 1) * body_own] = piece[k, :, star_own:]
            slot += 1
    n, count = stars_out.shape[1], bodies_out.shape[1]
    middle = center_of(stars_out[0:3, :], bodies_out[0:3, :])
    star_pos = stars_out[0:3, :] - middle
    scale = stars_out[7:8, :]
    from_ref[...] = distance_from(star_pos, scale, bridge_soft).T.astype(bf16)
    sum_ref[...] = rows(split_rows(star_pos), 16).astype(bf16)
    pull_ref[...] = jnp.zeros_like(pull_ref)
    ti = block_of(n, 1024)
    tj = block_of(body_own, 256)

    def one_block(j, multiply):
        lanes = pl.ds(j, tj)
        body_pos = bodies_out[0:3, lanes] - middle
        body_vel = bodies_out[3:6, lanes]
        mass = bodies_out[6:7, lanes]
        to = distance_to(body_pos).astype(bf16)
        moments = rows(parts(mass * body_pos, 3) + parts(mass, 3), 16).astype(bf16)
        push = jnp.zeros((16, tj), f32)
        for i in range(0, n, ti):
            weight = weights(from_ref[i : i + ti, :], to)
            push += multiply(sum_ref[:, i : i + ti], weight)
            pull_ref[:, i : i + ti] += dot_t(moments, weight.astype(bf16))
        body_vel = body_vel + (step_time / 2.0) * moment(push, body_pos)
        body_pos = body_pos + middle + step_time * body_vel
        bodies_out[0:3, lanes] = body_pos
        bodies_out[3:6, lanes] = body_vel

    for j in range(0, body_own, tj):
        one_block(j, dot_both)

    def other_block(k, carry):
        one_block(pl.multiple_of(k * tj, tj), dot_high)
        return carry

    lax.fori_loop(body_own // tj, count // tj, other_block, 0)
    pull = pull_ref[...]
    mass_sum = pull[9:10] + pull[10:11] + pull[11:12]
    pull_out[...] = (pull[0:3] + pull[3:6] + pull[6:9] - star_pos * mass_sum) / stars_out[6:7, :]
    pos_out[...] = bodies_out[0:3, :body_own]
    vel_out[...] = bodies_out[3:6, :body_own]


def first_kick(pieces, star_own):
    blocks = sum(piece.shape[0] for piece in pieces)
    body_own = pieces[0].shape[2] - star_own
    n, count = blocks * star_own, blocks * body_own
    pairs = n * count
    return pl.pallas_call(
        functools.partial(kick_kernel, star_own, len(pieces)),
        out_shape=[
            jax.ShapeDtypeStruct((8, n), f32),
            jax.ShapeDtypeStruct((8, count), f32),
            jax.ShapeDtypeStruct((3, n), f32),
            jax.ShapeDtypeStruct((3, body_own), f32),
            jax.ShapeDtypeStruct((3, body_own), f32),
        ],
        scratch_shapes=[
            pltpu.VMEM((n, 32), bf16),
            pltpu.VMEM((16, n), bf16),
            pltpu.VMEM((16, n), f32),
        ],
        compiler_params=pltpu.CompilerParams(vmem_limit_bytes=vmem_limit),
        cost_estimate=pl.CostEstimate(flops=40 * pairs, bytes_accessed=0, transcendentals=pairs),
    )(*pieces)


def pull_kernel(stars_ref, bodies_ref, pull_out):
    own, count = pull_out.shape[1], bodies_ref.shape[1]
    middle = center_of(stars_ref[0:3, :], bodies_ref[0:3, :])
    star_pos = stars_ref[0:3, :own] - middle
    source = distance_from(star_pos, stars_ref[7:8, :own], bridge_soft).T.astype(bf16)
    tj = block_of(count, 1024)

    def one_block(k, pull):
        lanes = pl.ds(pl.multiple_of(k * tj, tj), tj)
        body_pos = bodies_ref[0:3, lanes] - middle
        mass = bodies_ref[6:7, lanes]
        to = distance_to(body_pos).astype(bf16)
        moments = rows(parts(mass * body_pos, 3) + parts(mass, 3), 16).astype(bf16)
        return pull + dot_t(moments, weights(source, to).astype(bf16))

    pull = lax.fori_loop(0, count // tj, one_block, jnp.zeros((16, own), f32))
    mass_sum = pull[9:10] + pull[10:11] + pull[11:12]
    pull_out[...] = (pull[0:3] + pull[3:6] + pull[6:9] - star_pos * mass_sum) / stars_ref[
        6:7, :own
    ]


def second_pull(stars, bodies, own):
    pairs = own * bodies.shape[1]
    return pl.pallas_call(
        pull_kernel,
        out_shape=jax.ShapeDtypeStruct((3, own), f32),
        compiler_params=pltpu.CompilerParams(vmem_limit_bytes=vmem_limit),
        cost_estimate=pl.CostEstimate(flops=40 * pairs, bytes_accessed=0, transcendentals=pairs),
    )(stars, bodies)


def push_kernel(stars_ref, pos_ref, vel_ref, vel_out):
    n = stars_ref.shape[1]
    middle = center_of(stars_ref[0:3, :], pos_ref[...])
    star_pos = stars_ref[0:3, :] - middle
    body_pos = pos_ref[...] - middle
    source = distance_from(star_pos, stars_ref[7:8, :], bridge_soft).T.astype(bf16)
    to = distance_to(body_pos).astype(bf16)
    sums = rows(split_rows(star_pos), 16).astype(bf16)
    ti = block_of(n, 1024)
    push = jnp.zeros((16, body_pos.shape[1]), f32)
    for i in range(0, n, ti):
        push += dot_both(sums[:, i : i + ti], weights(source[i : i + ti], to))
    vel_out[...] = vel_ref[...] + (step_time / 2.0) * moment(push, body_pos)


def second_push(stars, body_pos, body_vel):
    pairs = stars.shape[1] * body_pos.shape[1]
    return pl.pallas_call(
        push_kernel,
        out_shape=jax.ShapeDtypeStruct(body_vel.shape, f32),
        compiler_params=pltpu.CompilerParams(vmem_limit_bytes=vmem_limit),
        cost_estimate=pl.CostEstimate(flops=40 * pairs, bytes_accessed=0, transcendentals=pairs),
    )(stars, body_pos, body_vel)


def swap(x, axis, bits):
    count = lax.axis_size(axis)
    return lax.ppermute(x, axis, [(i, i ^ bits) for i in range(count)])


def radices(count):
    steps, bit = [], 1
    if count.bit_length() % 2 == 0:
        steps.append((1,))
        bit = 2
    while bit < count:
        steps.append((bit, 2 * bit, 3 * bit))
        bit *= 4
    return steps


def gather_pieces(x, axis):
    pieces = [x[None]]
    for step in radices(lax.axis_size(axis)):
        if len(pieces) > 1:
            pieces = [jnp.concatenate(pieces, axis=0)]
        pieces = pieces + [swap(pieces[0], axis, bits) for bits in step]
    return pieces


def sum_pieces(x, axis):
    pieces = [x]
    for step in radices(lax.axis_size(axis)):
        while len(pieces) > 1:
            pieces = [a + b for a, b in zip(pieces[::2], pieces[1::2])]
        pieces = pieces + [swap(pieces[0], axis, bits) for bits in step]
    return pieces


def local(
    cluster_pos, cluster_vel, cluster_mass, galaxy_pos, galaxy_vel, galaxy_kind, species_mass
):
    own = cluster_pos.shape[1]
    total_stars = own * lax.axis_size("sub")
    total_bodies = galaxy_pos.shape[1] * lax.axis_size("sub") * lax.axis_size("grp")
    star_mass = cluster_mass / total_stars
    species = jnp.arange(species_mass.shape[0], dtype=jnp.int32)
    body_mass = (
        jnp.sum(
            jnp.where(galaxy_kind[None, :] == species[:, None], species_mass[:, None], 0.0), axis=0
        )
        / total_bodies
    )
    scale = jnp.exp(jnp.log(star_mass) * (-2.0 / 3.0))
    stars = jnp.concatenate([cluster_pos, cluster_vel, star_mass[None], scale[None]], axis=0)
    bodies = jnp.concatenate(
        [galaxy_pos, galaxy_vel, body_mass[None], jnp.zeros_like(body_mass)[None]], axis=0
    )
    pieces = gather_pieces(jnp.concatenate([stars, bodies], axis=1), "sub")
    all_stars, all_bodies, pull, body_pos, body_vel = first_kick(pieces, own)
    end_stars, end_pos, end_vel = hermite(all_stars, sum_pieces(pull, "grp"), own)
    pull = second_pull(end_stars, all_bodies, own)
    pulls = sum_pieces(pull, "grp")
    body_vel = second_push(end_stars, body_pos, body_vel)
    while len(pulls) > 1:
        pulls = [a + b for a, b in zip(pulls[::2], pulls[1::2])]
    return end_pos, end_vel + (step_time / 2.0) * pulls[0], body_pos, body_vel


def solution(mesh):
    return jax.shard_map(
        local,
        mesh=mesh,
        in_specs=(
            P(None, "sub"),
            P(None, "sub"),
            P("sub"),
            P(None, ("grp", "sub")),
            P(None, ("grp", "sub")),
            P(("grp", "sub")),
            P(),
        ),
        out_specs=(
            P(None, "sub"),
            P(None, "sub"),
            P(None, ("grp", "sub")),
            P(None, ("grp", "sub")),
        ),
        check_vma=False,
    )
```

```python
import functools

import jax
import jax.numpy as jnp
import numpy as np
from jax import lax
from jax.experimental import pallas as pl
from jax.experimental.pallas import tpu as pltpu
from jax.sharding import PartitionSpec as P

SUBSTEPS = 8

step_time = 0.5
bridge_soft = 0.01
cluster_soft = 0.0025
f32 = jnp.float32
bf16 = jnp.bfloat16
vmem_limit = 48 * 1024 * 1024


def parts(x, count):
    terms = []
    for _ in range(count):
        term = x.astype(bf16).astype(f32)
        terms.append(term)
        x = x - term
    return terms


def dot(a, b):
    return lax.dot_general(a, b, (((1,), (0,)), ((), ())), preferred_element_type=f32)


def dot_t(a, b):
    return lax.dot_general(a, b, (((1,), (1,)), ((), ())), preferred_element_type=f32)


def split(x):
    high = x.astype(bf16)
    return high, (x - high.astype(f32)).astype(bf16)


def block_of(count, most):
    size = most
    while count % size:
        size //= 2
    return size


def row_of(x):
    return lax.broadcasted_iota(jnp.int32, x.shape, 0)


def rot(x):
    return pltpu.roll(x, 4, 0)


def block(row, a, sa, b, sb):
    return jnp.where(row < 3, a, jnp.where(row == 3, sa, jnp.where(row < 7, b, sb)))


def constant_parts(value):
    terms = []
    for _ in range(3):
        term = float(np.asarray(value, bf16))
        terms.append(term)
        value -= term
    return terms


def fill(row, block, third, seventh):
    return jnp.where(row == 3, third, jnp.where(row == 7, seventh, block))


def grid_of(y):
    x = jnp.where(row_of(y) < 3, y, 0.0)
    grid = jnp.floor(x * 8.0 + 0.5) * 0.125
    rest = x - grid
    square = jnp.sum(grid * grid, axis=0, keepdims=True)
    return grid, rest, square, jnp.sum(rest * (grid + x), axis=0, keepdims=True)


def distance_rows(grid, rest, q, p, soften):
    row = row_of(grid)
    e = parts(rest, 3)
    f = [-2.0 * term for term in e]
    soft = constant_parts(soften)
    twice = -2.0 * grid
    rot_grid, rot_twice = rot(grid), rot(twice)
    rot_e, rot_f = rot(e[1]), rot(f[0])
    targets = [
        block(row, grid, q[0], jnp.where(row == 4, q[1], 1.0), 1.0),
        block(row, e[0], p[0], rot_e, p[1]),
        block(row, e[2], p[2], rot_grid, 1.0),
        block(row, grid, 1.0, rot_grid, 1.0),
        block(row, e[0], 1.0, rot_e, 1.0),
        e[0],
    ]
    last = jnp.where(row == 4, 1.0, jnp.where(row == 5, q[0], q[1]))
    sources = [
        block(row, twice, 1.0, last, soft[0]),
        block(row, twice, 1.0, rot_twice, 1.0),
        block(row, twice, 1.0, rot_f, p[0]),
        block(row, f[1], p[1], rot(f[2]), p[2]),
        block(row, f[0], soft[1], rot_f, soft[2]),
        f[1],
    ]
    return jnp.concatenate(sources, axis=0), jnp.concatenate(targets, axis=0)


def distance_blocks(y, soften):
    grid, rest, square, small = grid_of(y)
    return distance_rows(grid, rest, parts(square, 2), parts(small, 3), soften)


def phase_blocks(y):
    row = row_of(y)
    grid, rest, square, small = grid_of(y)
    product = jnp.sum(jnp.where(row < 3, y * rot(y), 0.0), axis=0, keepdims=True)
    scalars = parts(jnp.where(row == 0, square, jnp.where(row == 1, small, -product)), 3)
    q = [term[0:1] for term in scalars]
    p = [term[1:2] for term in scalars]
    c = [term[2:3] for term in scalars]
    source, target = distance_rows(grid, rest, q, p, cluster_soft)
    y1, y2, y3 = parts(y, 3)
    r1, r2, r3 = rot(y1), rot(y2), rot(y3)
    sources = [
        fill(row, y1, 1.0, c[0]),
        fill(row, y1, 1.0, c[1]),
        fill(row, y2, 1.0, c[2]),
        y2,
        y1,
        y3,
    ]
    targets = [
        fill(row, r1, c[0], 1.0),
        fill(row, r2, c[1], 1.0),
        fill(row, r1, c[2], 1.0),
        r2,
        r3,
        r1,
    ]
    sums = [
        fill(row, y1, 1.0, pltpu.roll(y3, 7, 0)),
        fill(row, y2, pltpu.roll(y3, 2, 0), pltpu.roll(y3, 5, 0)),
    ]
    return (
        jnp.concatenate([source] + sources, axis=0).astype(bf16),
        target.astype(bf16),
        jnp.concatenate(targets, axis=0).astype(bf16),
        jnp.concatenate(sums, axis=0).astype(bf16),
    )


def phase_moment(first, second, y):
    row = row_of(y)
    third = jnp.where(
        row == 0,
        pltpu.roll(first, 1, 0),
        jnp.where(
            row == 1, pltpu.roll(second, 6, 0), jnp.where(row == 2, pltpu.roll(second, 3, 0), 0.0)
        ),
    )
    return first + jnp.where(row == 3, 0.0, second) + third - y * first[3:4]


def mass_rows(y, mass):
    row = row_of(y)
    terms = parts(jnp.where(row < 3, mass * y, jnp.where(row == 3, mass, 0.0)), 3)
    return jnp.concatenate([terms[0] + rot(terms[1]), terms[2]], axis=0).astype(bf16)


def mass_moment(total, y):
    total = total[0:8] + rot(total[0:8]) + total[8:16]
    return jnp.where(row_of(y) < 3, total - y * total[3:4], 0.0)


def mean_of(y):
    mean = jnp.mean(y, axis=1, keepdims=True)
    return jnp.where(row_of(mean) < 3, mean, 0.0)


def weights(sources, targets):
    inverse = lax.rsqrt(dot(sources, targets))
    return inverse * inverse * inverse


def evaluate(y, mass_ref, refs):
    from_ref, to_ref, phase_ref, sum_ref = refs
    n = y.shape[1]
    row = row_of(y)
    y = fill(row, y, 0.0, 0.0)
    source, distance, closing, phase = phase_blocks(y)
    from_ref[...] = source.T
    phase_ref[...] = phase
    ti, tj = block_of(n, 1024), block_of(n, 128)
    for j in range(0, n, tj):
        to_ref[0:48, 2 * j : 2 * j + tj] = distance[:, j : j + tj]
        to_ref[48:96, 2 * j + tj : 2 * j + 2 * tj] = closing[:, j : j + tj]

    def weight_block(across, j):
        both = dot(from_ref[across, :], to_ref[:, pl.ds(2 * j, 2 * tj)])
        inverse = lax.rsqrt(both[:, :tj])
        square = inverse * inverse
        mass = jnp.concatenate([mass_ref[across, :]] * (tj // 128), axis=1)
        weight = square * (inverse * mass)
        radial = weight * square * both[:, tj:]
        return jnp.concatenate(
            [
                jnp.concatenate(split(weight), axis=0),
                jnp.concatenate(split(radial), axis=0),
            ],
            axis=1,
        )

    def sums(across, both):
        phase = phase_ref[:, across]
        return dot(jnp.concatenate([phase, phase], axis=1), both)

    def store(j, total):
        sum_ref[0:16, pl.ds(j, tj)] = total[:, :tj]
        sum_ref[16:32, pl.ds(j, tj)] = total[:, tj:]

    if n == ti:
        every = slice(0, n)
        waiting = None
        for j in range(0, n, tj):
            both = weight_block(every, j)
            if waiting is not None:
                store(j - tj, sums(every, waiting))
            waiting = both
        store(n - tj, sums(every, waiting))
    else:

        def one_block(k, carry):
            j = pl.multiple_of(k * tj, tj)
            total = jnp.zeros((16, 2 * tj), f32)
            for i in range(0, n, ti):
                across = slice(i, i + ti)
                total += sums(across, weight_block(across, j))
            store(j, total)
            return carry

        lax.fori_loop(0, n // tj, one_block, 0)
    direct = phase_moment(sum_ref[0:8, :], sum_ref[8:16, :], y)
    radial = phase_moment(sum_ref[16:24, :], sum_ref[24:32, :], y)
    return direct + jnp.where(row >= 4, 3.0 * rot(radial), 0.0)


def add_up(values):
    while len(values) > 1:
        values = [a + b for a, b in zip(values[::2], values[1::2])]
    return values[0]


def hermite_kernel(pull_count, stars_ref, center_ref, targets_ref, body_rows_ref, *refs):
    pulls, (stars_out, pos_out, vel_out, pull_out, mass_ref, *work) = (
        refs[:pull_count],
        refs[pull_count:],
    )
    own, count = pos_out.shape[1], targets_ref.shape[1]
    stars = stars_ref[...]
    n = stars.shape[1]
    row = row_of(stars)
    mass_ref[...] = jnp.broadcast_to(stars[3:4, :], (128, n)).T
    work[1][...] = jnp.zeros_like(work[1])
    pull = add_up([ref[...] for ref in pulls])
    y = jnp.where(row == 3, 0.0, stars)
    y = y + (step_time / 2.0) * jnp.concatenate([jnp.zeros_like(pull), pull], axis=0)
    frame = jnp.mean(y, axis=1, keepdims=True)
    y = y - frame
    h = step_time / SUBSTEPS
    pos_row, vel_row = row < 3, row >= 4
    guess_vel = jnp.where(pos_row, h, 0.0)
    guess_other = jnp.where(pos_row, h * h * h / 6.0, h)
    kick = jnp.where(vel_row, h / 2.0, 0.0)
    drift = jnp.where(pos_row, h / 2.0, 0.0)
    rates = evaluate(y, mass_ref, work)

    def substep(_, carry):
        y, rates = carry
        vel = rot(y)
        guess = y + guess_vel * vel + (h * h / 2.0) * rates + guess_other * rot(rates)
        fresh = evaluate(guess, mass_ref, work)
        z = y + (h * h / 12.0) * (rates - fresh) + kick * rot(rates + fresh)
        return z + drift * (vel + rot(z)), fresh

    y, _ = lax.fori_loop(0, SUBSTEPS, substep, (y, rates))
    frame = frame + jnp.where(row_of(frame) < 3, step_time * jnp.concatenate([frame[4:8], frame[0:4]], axis=0), 0.0)
    y = y + frame
    stars_out[...] = jnp.where(row == 3, stars, y)
    y = y[:, :own]
    pos_out[...] = y[0:3]
    vel_out[...] = y[4:7]
    y = y - center_ref[:, 0:1]
    source = distance_blocks(y, bridge_soft)[0].astype(bf16).T
    tj = block_of(count, 2048)
    total = jnp.zeros((16, own), f32)
    for j in range(0, count, tj):
        weight = weights(source, targets_ref[:, j : j + tj]).astype(bf16)
        total += dot_t(body_rows_ref[:, j : j + tj], weight)
    pull_out[...] = mass_moment(total, y)[0:3]


def hermite(stars, center, body_targets, body_rows, pulls, own):
    n = stars.shape[1]
    pairs = n * n * (SUBSTEPS + 1)
    return pl.pallas_call(
        functools.partial(hermite_kernel, len(pulls)),
        out_shape=[
            jax.ShapeDtypeStruct(stars.shape, f32),
            jax.ShapeDtypeStruct((3, own), f32),
            jax.ShapeDtypeStruct((3, own), f32),
            jax.ShapeDtypeStruct((3, own), f32),
        ],
        scratch_shapes=[
            pltpu.VMEM((n, 128), f32),
            pltpu.VMEM((n, 96), bf16),
            pltpu.VMEM((96, 2 * n), bf16),
            pltpu.VMEM((16, n), bf16),
            pltpu.VMEM((32, n), f32),
        ],
        compiler_params=pltpu.CompilerParams(vmem_limit_bytes=vmem_limit),
        cost_estimate=pl.CostEstimate(flops=80 * pairs, bytes_accessed=0, transcendentals=pairs),
    )(stars, center, body_targets, body_rows, *pulls)


def sweep(start, stop, step, body):
    if (stop - start) // step <= 8:
        for j in range(start, stop, step):
            body(j)
        return

    def one(k, carry):
        body(pl.multiple_of(start + k * step, step))
        return carry

    lax.fori_loop(0, (stop - start) // step, one, 0)


def kick_kernel(star_own, before, piece_count, *refs):
    pieces, refs = refs[:piece_count], refs[piece_count:]
    held, refs = (refs[:9], refs[9:]) if before else (None, refs)
    outs, (pull_ref, push_ref) = refs[:9], refs[9:]
    center, stars, bodies, source, target, star_rows, body_rows, push, pull = outs
    body_own = pieces[0].shape[2] - star_own
    n, count = stars.shape[1], bodies.shape[1]
    n_held = count_held = 0
    if before:
        n_held, count_held = held[1].shape[1], held[2].shape[1]
        center[...] = held[0][...]
        source[:n_held, :] = held[3][...]
        for old, ref in ((held[1], stars), (held[5], star_rows)):
            ref[:, :n_held] = old[...]
        for old, ref in ((held[2], bodies), (held[4], target), (held[6], body_rows)):
            ref[:, :count_held] = old[...]
    slot = n_held // star_own
    for piece in pieces:
        for k in range(piece.shape[0]):
            stars[:, slot * star_own : (slot + 1) * star_own] = piece[k, :, :star_own]
            bodies[:, slot * body_own : (slot + 1) * body_own] = piece[k, :, star_own:]
            slot += 1
    if not before:
        center[...] = jnp.broadcast_to(mean_of(stars[...]), center.shape)
    middle = center[:, 0:1]
    y = stars[:, n_held:] - middle
    source[n_held:, :] = distance_blocks(y, bridge_soft)[0].astype(bf16).T
    star_rows[:, n_held:] = mass_rows(y, stars[3:4, n_held:])
    x = bodies[:, count_held:] - middle
    target[:, count_held:] = distance_blocks(x, bridge_soft)[1].astype(bf16)
    body_rows[:, count_held:] = mass_rows(x, bodies[3:4, count_held:])
    pull_ref[...] = jnp.zeros_like(pull_ref)
    push_ref[...] = jnp.zeros_like(push_ref)
    tj = block_of(body_own, 256)

    def rectangle(first, last, width, exact, j):
        lanes = pl.ds(j, width)
        ti = block_of(last - first, 1024)
        for i in range(first, last, ti):
            across = slice(i, i + ti)
            high, low = split(weights(source[across, :], target[:, lanes]))
            total = dot(star_rows[:, across], high)
            if exact:
                total += dot(star_rows[:, across], low)
            push_ref[:, lanes] += total
            pull_ref[:, across] += dot_t(body_rows[:, lanes], high)

    def all_pairs(first, last, start, stop, exact):
        if stop > start:
            width = block_of(stop - start, 512)
            sweep(start, stop, width, functools.partial(rectangle, first, last, width, exact))

    if before:
        all_pairs(n_held, n, 0, body_own, True)
        all_pairs(n_held, n, body_own, count_held, False)
        all_pairs(0, n, count_held, count, False)
    else:
        all_pairs(0, n, 0, body_own, True)
        all_pairs(0, n, body_own, count, False)
    total = mass_moment(push_ref[...], bodies[...] - middle)
    push[...] = total
    pull[...] = mass_moment(pull_ref[...], stars[...] - middle)[0:4]
    if before:
        push[:, :count_held] = held[7][...] + total[:, :count_held]
        pull[:, :n_held] = held[8][...] + pull[:, :n_held]


def kick(held, pieces, star_own):
    blocks = sum(piece.shape[0] for piece in pieces)
    body_own = pieces[0].shape[2] - star_own
    new = blocks * blocks
    if held:
        old = held[1].shape[1] // star_own
        new += 2 * old * blocks
        blocks += old
    n, count = blocks * star_own, blocks * body_own
    pairs = new * star_own * body_own
    shapes = [
        ((8, 128), f32),
        ((8, n), f32),
        ((8, count), f32),
        ((n, 48), bf16),
        ((48, count), bf16),
        ((16, n), bf16),
        ((16, count), bf16),
        ((8, count), f32),
        ((4, n), f32),
    ]
    return pl.pallas_call(
        functools.partial(kick_kernel, star_own, bool(held), len(pieces)),
        out_shape=[jax.ShapeDtypeStruct(*shape) for shape in shapes],
        scratch_shapes=[pltpu.VMEM((16, n), f32), pltpu.VMEM((16, count), f32)],
        compiler_params=pltpu.CompilerParams(vmem_limit_bytes=vmem_limit),
        cost_estimate=pl.CostEstimate(flops=40 * pairs, bytes_accessed=0, transcendentals=pairs),
    )(*pieces, *held)


def first_kick(x, axis, star_own):
    pieces = gather_pieces(x, axis)
    held = kick([], pieces[:2], star_own)
    for piece in pieces[2:]:
        held = kick(held, [piece], star_own)
    _, stars, bodies, _, _, _, _, push, pull = held
    return stars, bodies, push, pull


def drift_kernel(bodies_ref, push_ref, pos_out, vel_out, center_out, targets_out, rows_out):
    own = pos_out.shape[1]
    bodies = bodies_ref[...]
    row = row_of(bodies)
    moved = bodies + (step_time / 2.0) * rot(push_ref[...])
    moved = moved + jnp.where(row < 3, step_time * rot(moved), 0.0)
    pos_out[...] = moved[0:3, :own]
    vel_out[...] = moved[4:7, :own]
    middle = mean_of(moved)
    center_out[...] = jnp.broadcast_to(middle, center_out.shape)
    x = moved - middle
    targets_out[...] = distance_blocks(x, bridge_soft)[1].astype(bf16)
    rows_out[...] = mass_rows(x, bodies[3:4, :])


def drift(bodies, push, own):
    count = bodies.shape[1]
    return pl.pallas_call(
        drift_kernel,
        out_shape=[
            jax.ShapeDtypeStruct((3, own), f32),
            jax.ShapeDtypeStruct((3, own), f32),
            jax.ShapeDtypeStruct((8, 128), f32),
            jax.ShapeDtypeStruct((48, count), bf16),
            jax.ShapeDtypeStruct((16, count), bf16),
        ],
        compiler_params=pltpu.CompilerParams(vmem_limit_bytes=vmem_limit),
        cost_estimate=pl.CostEstimate(
            flops=2000 * count, bytes_accessed=200 * count, transcendentals=0
        ),
    )(bodies, push)


def push_kernel(stars_ref, center_ref, targets_ref, pos_ref, vel_ref, vel_out):
    own = vel_out.shape[1]
    stars = stars_ref[...]
    n = stars.shape[1]
    y = stars - center_ref[:, 0:1]
    source = distance_blocks(y, bridge_soft)[0].astype(bf16).T
    star_rows = mass_rows(y, stars[3:4, :])
    ti, tj = block_of(n, 1024), block_of(own, 256)
    for j in range(0, own, tj):
        total = jnp.zeros((16, tj), f32)
        for i in range(0, n, ti):
            high, low = split(weights(source[i : i + ti, :], targets_ref[:, j : j + tj]))
            total += dot(star_rows[:, i : i + ti], high) + dot(star_rows[:, i : i + ti], low)
        x = pos_ref[:, j : j + tj] - center_ref[0:3, 0:1]
        x = jnp.concatenate([x, jnp.zeros((5, tj), f32)], axis=0)
        push = mass_moment(total, x)[0:3]
        vel_out[:, j : j + tj] = vel_ref[:, j : j + tj] + (step_time / 2.0) * push


def second_push(stars, center, targets, pos, vel):
    pairs = stars.shape[1] * pos.shape[1]
    return pl.pallas_call(
        push_kernel,
        grid=(1,),
        in_specs=[
            pl.BlockSpec(stars.shape, lambda i: (0, 0)),
            pl.BlockSpec(center.shape, lambda i: (0, 0)),
            pl.BlockSpec((48, pos.shape[1]), lambda i: (0, 0)),
            pl.BlockSpec(pos.shape, lambda i: (0, 0)),
            pl.BlockSpec(vel.shape, lambda i: (0, 0)),
        ],
        out_specs=pl.BlockSpec(vel.shape, lambda i: (0, 0)),
        out_shape=jax.ShapeDtypeStruct(vel.shape, f32),
        compiler_params=pltpu.CompilerParams(vmem_limit_bytes=vmem_limit),
        cost_estimate=pl.CostEstimate(flops=40 * pairs, bytes_accessed=0, transcendentals=pairs),
    )(stars, center, targets, pos, vel)


def prepare_kernel(
    total_stars, total_bodies, species, pos, vel, mass, body_pos, body_vel, kind, out
):
    own = pos.shape[1]
    out[0:3, :own] = pos[...]
    out[3:4, :own] = mass[...] / total_stars
    out[4:7, :own] = vel[...]
    out[7:8, :] = jnp.zeros_like(out[7:8, :])
    body_mass = jnp.zeros(kind.shape, f32)
    for k in range(species.shape[1]):
        body_mass = body_mass + jnp.where(kind[...] == k, species[:, k : k + 1], 0.0)
    out[0:3, own:] = body_pos[...]
    out[3:4, own:] = body_mass / total_bodies
    out[4:7, own:] = body_vel[...]


def prepare(species, pos, vel, mass, body_pos, body_vel, kind, total_stars, total_bodies):
    whole = pl.BlockSpec(memory_space=pltpu.VMEM)
    return pl.pallas_call(
        functools.partial(prepare_kernel, total_stars, total_bodies),
        in_specs=[whole] * 7,
        out_specs=whole,
        out_shape=jax.ShapeDtypeStruct((8, pos.shape[1] + body_pos.shape[1]), f32),
    )(species[None], pos, vel, mass[None], body_pos, body_vel, kind[None])


def swap(x, axis, bits):
    count = lax.axis_size(axis)
    return lax.ppermute(x, axis, [(i, i ^ bits) for i in range(count)])


def radices(count):
    steps, bit = [], 1
    if count.bit_length() % 2 == 0:
        steps.append((1,))
        bit = 2
    while bit < count:
        steps.append((bit, 2 * bit, 3 * bit))
        bit *= 4
    return steps


def gather_pieces(x, axis):
    pieces = [x[None]]
    for step in radices(lax.axis_size(axis)):
        if len(pieces) > 1:
            pieces = [jnp.concatenate(pieces, axis=0)]
        pieces = pieces + [swap(pieces[0], axis, bits) for bits in step]
    return pieces


def sum_pieces(x, axis):
    pieces = [x]
    for step in radices(lax.axis_size(axis)):
        while len(pieces) > 1:
            pieces = [a + b for a, b in zip(pieces[::2], pieces[1::2])]
        pieces = pieces + [swap(pieces[0], axis, bits) for bits in step]
    return pieces


def local(
    cluster_pos, cluster_vel, cluster_mass, galaxy_pos, galaxy_vel, galaxy_kind, species_mass
):
    own = cluster_pos.shape[1]
    total_stars = own * lax.axis_size("sub")
    total_bodies = galaxy_pos.shape[1] * lax.axis_size("sub") * lax.axis_size("grp")
    block = prepare(
        species_mass,
        cluster_pos,
        cluster_vel,
        cluster_mass,
        galaxy_pos,
        galaxy_vel,
        galaxy_kind,
        total_stars,
        total_bodies,
    )
    stars, bodies, push, pull = first_kick(block, "sub", own)
    pulls = sum_pieces(pull, "grp")
    body_pos, body_vel, center, targets, body_rows = drift(bodies, push, galaxy_pos.shape[1])
    stars, end_pos, end_vel, pull = hermite(stars, center, targets, body_rows, pulls, own)
    pull = add_up(sum_pieces(pull, "grp"))
    body_vel = second_push(stars, center, targets, body_pos, body_vel)
    return end_pos, end_vel + (step_time / 2.0) * pull, body_pos, body_vel


def solution(mesh):
    return jax.shard_map(
        local,
        mesh=mesh,
        in_specs=(
            P(None, "sub"),
            P(None, "sub"),
            P("sub"),
            P(None, ("grp", "sub")),
            P(None, ("grp", "sub")),
            P(("grp", "sub")),
            P(),
        ),
        out_specs=(
            P(None, "sub"),
            P(None, "sub"),
            P(None, ("grp", "sub")),
            P(None, ("grp", "sub")),
        ),
        check_vma=False,
    )
```

```python
import functools

import jax
import jax.numpy as jnp
import numpy as np
from jax import lax
from jax.experimental import pallas as pl
from jax.experimental.pallas import tpu as pltpu
from jax.sharding import PartitionSpec as P

SUBSTEPS = 8

step_time = 0.5
bridge_soft = 0.01
cluster_soft = 0.0025
f32 = jnp.float32
bf16 = jnp.bfloat16
vmem_limit = 48 * 1024 * 1024


def parts(x, count):
    terms = []
    for _ in range(count):
        term = x.astype(bf16).astype(f32)
        terms.append(term)
        x = x - term
    return terms


def dot(a, b):
    return lax.dot_general(a, b, (((1,), (0,)), ((), ())), preferred_element_type=f32)


def dot_t(a, b):
    return lax.dot_general(a, b, (((1,), (1,)), ((), ())), preferred_element_type=f32)


def split(x):
    high = x.astype(bf16)
    return high, (x - high.astype(f32)).astype(bf16)


def block_of(count, most):
    size = most
    while count % size:
        size //= 2
    return size


def row_of(x):
    return lax.broadcasted_iota(jnp.int32, x.shape, 0)


def rot(x):
    return pltpu.roll(x, 4, 0)


def block(row, a, sa, b, sb):
    return jnp.where(row < 3, a, jnp.where(row == 3, sa, jnp.where(row < 7, b, sb)))


def constant_parts(value):
    terms = []
    for _ in range(3):
        term = float(np.asarray(value, bf16))
        terms.append(term)
        value -= term
    return terms


def fill(row, block, third, seventh):
    return jnp.where(row == 3, third, jnp.where(row == 7, seventh, block))


def grid_of(y):
    x = jnp.where(row_of(y) < 3, y, 0.0)
    grid = jnp.floor(x * 8.0 + 0.5) * 0.125
    rest = x - grid
    square = jnp.sum(grid * grid, axis=0, keepdims=True)
    return grid, rest, square, jnp.sum(rest * (grid + x), axis=0, keepdims=True)


def distance_rows(grid, rest, q, p, soften):
    row = row_of(grid)
    e = parts(rest, 3)
    f = [-2.0 * term for term in e]
    soft = constant_parts(soften)
    twice = -2.0 * grid
    rot_grid, rot_twice = rot(grid), rot(twice)
    rot_e, rot_f = rot(e[1]), rot(f[0])
    targets = [
        block(row, grid, q[0], jnp.where(row == 4, q[1], 1.0), 1.0),
        block(row, e[0], p[0], rot_e, p[1]),
        block(row, e[2], p[2], rot_grid, 1.0),
        block(row, grid, 1.0, rot_grid, 1.0),
        block(row, e[0], 1.0, rot_e, 1.0),
        e[0],
    ]
    last = jnp.where(row == 4, 1.0, jnp.where(row == 5, q[0], q[1]))
    sources = [
        block(row, twice, 1.0, last, soft[0]),
        block(row, twice, 1.0, rot_twice, 1.0),
        block(row, twice, 1.0, rot_f, p[0]),
        block(row, f[1], p[1], rot(f[2]), p[2]),
        block(row, f[0], soft[1], rot_f, soft[2]),
        f[1],
    ]
    return jnp.concatenate(sources, axis=0), jnp.concatenate(targets, axis=0)


def distance_blocks(y, soften):
    grid, rest, square, small = grid_of(y)
    return distance_rows(grid, rest, parts(square, 2), parts(small, 3), soften)


def phase_blocks(y):
    row = row_of(y)
    grid, rest, square, small = grid_of(y)
    product = jnp.sum(jnp.where(row < 3, y * rot(y), 0.0), axis=0, keepdims=True)
    scalars = parts(jnp.where(row == 0, square, jnp.where(row == 1, small, -product)), 3)
    q = [term[0:1] for term in scalars]
    p = [term[1:2] for term in scalars]
    c = [term[2:3] for term in scalars]
    source, target = distance_rows(grid, rest, q, p, cluster_soft)
    y1, y2, y3 = parts(y, 3)
    r1, r2, r3 = rot(y1), rot(y2), rot(y3)
    sources = [
        fill(row, y1, 1.0, c[0]),
        fill(row, y1, 1.0, c[1]),
        fill(row, y2, 1.0, c[2]),
        y2,
        y1,
        y3,
    ]
    targets = [
        fill(row, r1, c[0], 1.0),
        fill(row, r2, c[1], 1.0),
        fill(row, r1, c[2], 1.0),
        r2,
        r3,
        r1,
    ]
    sums = [
        fill(row, y1, 1.0, pltpu.roll(y3, 7, 0)),
        fill(row, y2, pltpu.roll(y3, 2, 0), pltpu.roll(y3, 5, 0)),
    ]
    return (
        jnp.concatenate([source] + sources, axis=0).astype(bf16),
        target.astype(bf16),
        jnp.concatenate(targets, axis=0).astype(bf16),
        jnp.concatenate(sums, axis=0).astype(bf16),
    )


def phase_moment(first, second, y):
    row = row_of(y)
    third = jnp.where(
        row == 0,
        pltpu.roll(first, 1, 0),
        jnp.where(
            row == 1, pltpu.roll(second, 6, 0), jnp.where(row == 2, pltpu.roll(second, 3, 0), 0.0)
        ),
    )
    return first + jnp.where(row == 3, 0.0, second) + third - y * first[3:4]


def mass_rows(y, mass):
    row = row_of(y)
    terms = parts(jnp.where(row < 3, mass * y, jnp.where(row == 3, mass, 0.0)), 3)
    return jnp.concatenate([terms[0] + rot(terms[1]), terms[2]], axis=0).astype(bf16)


def mass_moment(total, y):
    total = total[0:8] + rot(total[0:8]) + total[8:16]
    return jnp.where(row_of(y) < 3, total - y * total[3:4], 0.0)


def mean_of(y):
    mean = jnp.mean(y, axis=1, keepdims=True)
    return jnp.where(row_of(mean) < 3, mean, 0.0)


def weights(sources, targets):
    inverse = lax.rsqrt(dot(sources, targets))
    return inverse * inverse * inverse


def evaluate(y, mass_ref, refs):
    from_ref, to_ref, phase_ref, sum_ref = refs
    n = y.shape[1]
    row = row_of(y)
    y = fill(row, y, 0.0, 0.0)
    source, distance, closing, phase = phase_blocks(y)
    from_ref[...] = source.T
    phase_ref[...] = phase
    ti, tj = block_of(n, 1024), block_of(n, 128)
    for j in range(0, n, tj):
        to_ref[0:48, 2 * j : 2 * j + tj] = distance[:, j : j + tj]
        to_ref[48:96, 2 * j + tj : 2 * j + 2 * tj] = closing[:, j : j + tj]

    def weight_block(across, j):
        both = dot(from_ref[across, :], to_ref[:, pl.ds(2 * j, 2 * tj)])
        inverse = lax.rsqrt(both[:, :tj])
        square = inverse * inverse
        mass = jnp.concatenate([mass_ref[across, :]] * (tj // 128), axis=1)
        weight = square * (inverse * mass)
        radial = weight * square * both[:, tj:]
        return jnp.concatenate(
            [
                jnp.concatenate(split(weight), axis=0),
                jnp.concatenate(split(radial), axis=0),
            ],
            axis=1,
        )

    def sums(across, both):
        phase = phase_ref[:, across]
        return dot(jnp.concatenate([phase, phase], axis=1), both)

    def store(j, total):
        sum_ref[0:16, pl.ds(j, tj)] = total[:, :tj]
        sum_ref[16:32, pl.ds(j, tj)] = total[:, tj:]

    if n == ti:
        every = slice(0, n)
        waiting = None
        for j in range(0, n, tj):
            both = weight_block(every, j)
            if waiting is not None:
                store(j - tj, sums(every, waiting))
            waiting = both
        store(n - tj, sums(every, waiting))
    else:

        def one_block(k, carry):
            j = pl.multiple_of(k * tj, tj)
            total = jnp.zeros((16, 2 * tj), f32)
            for i in range(0, n, ti):
                across = slice(i, i + ti)
                total += sums(across, weight_block(across, j))
            store(j, total)
            return carry

        lax.fori_loop(0, n // tj, one_block, 0)
    direct = phase_moment(sum_ref[0:8, :], sum_ref[8:16, :], y)
    radial = phase_moment(sum_ref[16:24, :], sum_ref[24:32, :], y)
    return direct + jnp.where(row >= 4, 3.0 * rot(radial), 0.0)


def add_up(values):
    while len(values) > 1:
        values = [a + b for a, b in zip(values[::2], values[1::2])]
    return values[0]


def hermite_kernel(pull_count, stars_ref, center_ref, targets_ref, body_rows_ref, *refs):
    pulls, (stars_out, pos_out, vel_out, pull_out, mass_ref, *work) = (
        refs[:pull_count],
        refs[pull_count:],
    )
    own, count = pos_out.shape[1], targets_ref.shape[1]
    stars = stars_ref[...]
    n = stars.shape[1]
    row = row_of(stars)
    mass_ref[...] = jnp.broadcast_to(stars[3:4, :], (128, n)).T
    work[1][...] = jnp.zeros_like(work[1])
    pull = add_up([ref[...] for ref in pulls])
    y = jnp.where(row == 3, 0.0, stars)
    y = y + (step_time / 2.0) * jnp.concatenate([jnp.zeros_like(pull), pull], axis=0)
    frame = jnp.mean(y, axis=1, keepdims=True)
    y = y - frame
    h = step_time / SUBSTEPS
    pos_row, vel_row = row < 3, row >= 4
    guess_vel = jnp.where(pos_row, h, 0.0)
    guess_other = jnp.where(pos_row, h * h * h / 6.0, h)
    kick = jnp.where(vel_row, h / 2.0, 0.0)
    drift = jnp.where(pos_row, h / 2.0, 0.0)
    rates = evaluate(y, mass_ref, work)

    def substep(_, carry):
        y, rates = carry
        vel = rot(y)
        guess = y + guess_vel * vel + (h * h / 2.0) * rates + guess_other * rot(rates)
        fresh = evaluate(guess, mass_ref, work)
        z = y + (h * h / 12.0) * (rates - fresh) + kick * rot(rates + fresh)
        return z + drift * (vel + rot(z)), fresh

    y, _ = lax.fori_loop(0, SUBSTEPS, substep, (y, rates))
    frame = frame + jnp.where(row_of(frame) < 3, step_time * jnp.concatenate([frame[4:8], frame[0:4]], axis=0), 0.0)
    y = y + frame
    stars_out[...] = jnp.where(row == 3, stars, y)
    y = y[:, :own]
    pos_out[...] = y[0:3]
    vel_out[...] = y[4:7]
    y = y - center_ref[:, 0:1]
    source = distance_blocks(y, bridge_soft)[0].astype(bf16).T
    tj = block_of(count, 2048)
    total = jnp.zeros((16, own), f32)
    for j in range(0, count, tj):
        weight = weights(source, targets_ref[:, j : j + tj]).astype(bf16)
        total += dot_t(body_rows_ref[:, j : j + tj], weight)
    pull_out[...] = mass_moment(total, y)[0:3]


def hermite(stars, center, body_targets, body_rows, pulls, own):
    n = stars.shape[1]
    pairs = n * n * (SUBSTEPS + 1)
    return pl.pallas_call(
        functools.partial(hermite_kernel, len(pulls)),
        out_shape=[
            jax.ShapeDtypeStruct(stars.shape, f32),
            jax.ShapeDtypeStruct((3, own), f32),
            jax.ShapeDtypeStruct((3, own), f32),
            jax.ShapeDtypeStruct((3, own), f32),
        ],
        scratch_shapes=[
            pltpu.VMEM((n, 128), f32),
            pltpu.VMEM((n, 96), bf16),
            pltpu.VMEM((96, 2 * n), bf16),
            pltpu.VMEM((16, n), bf16),
            pltpu.VMEM((32, n), f32),
        ],
        compiler_params=pltpu.CompilerParams(vmem_limit_bytes=vmem_limit),
        cost_estimate=pl.CostEstimate(flops=80 * pairs, bytes_accessed=0, transcendentals=pairs),
    )(stars, center, body_targets, body_rows, *pulls)


def sweep(start, stop, step, body):
    if (stop - start) // step <= 8:
        for j in range(start, stop, step):
            body(j)
        return

    def one(k, carry):
        body(pl.multiple_of(start + k * step, step))
        return carry

    lax.fori_loop(0, (stop - start) // step, one, 0)


def kick_kernel(star_own, before, last, piece_count, *refs):
    pieces, refs = refs[:piece_count], refs[piece_count:]
    held, refs = (refs[:9], refs[9:]) if before else (None, refs)
    if last:
        stars, bodies, push, pull, center, source, target, star_rows, body_rows = refs[:9]
    else:
        center, stars, bodies, source, target, star_rows, body_rows, push, pull = refs[:9]
    pull_ref, push_ref = refs[9:]
    body_own = pieces[0].shape[2] - star_own
    n, count = stars.shape[1], bodies.shape[1]
    n_held = count_held = 0
    if before:
        n_held, count_held = held[1].shape[1], held[2].shape[1]
        center[...] = held[0][...]
        source[:n_held, :] = held[3][...]
        for old, ref in ((held[1], stars), (held[5], star_rows)):
            ref[:, :n_held] = old[...]
        for old, ref in ((held[2], bodies), (held[4], target), (held[6], body_rows)):
            ref[:, :count_held] = old[...]
    slot = n_held // star_own
    for piece in pieces:
        for k in range(piece.shape[0]):
            stars[:, slot * star_own : (slot + 1) * star_own] = piece[k, :, :star_own]
            bodies[:, slot * body_own : (slot + 1) * body_own] = piece[k, :, star_own:]
            slot += 1
    if not before:
        center[...] = jnp.broadcast_to(mean_of(stars[...]), center.shape)
    middle = center[:, 0:1]
    y = stars[:, n_held:] - middle
    source[n_held:, :] = distance_blocks(y, bridge_soft)[0].astype(bf16).T
    star_rows[:, n_held:] = mass_rows(y, stars[3:4, n_held:])
    x = bodies[:, count_held:] - middle
    target[:, count_held:] = distance_blocks(x, bridge_soft)[1].astype(bf16)
    body_rows[:, count_held:] = mass_rows(x, bodies[3:4, count_held:])
    pull_ref[...] = jnp.zeros_like(pull_ref)
    push_ref[...] = jnp.zeros_like(push_ref)
    tj = block_of(body_own, 256)

    def rectangle(first, last, width, exact, j):
        lanes = pl.ds(j, width)
        ti = block_of(last - first, 1024)
        for i in range(first, last, ti):
            across = slice(i, i + ti)
            high, low = split(weights(source[across, :], target[:, lanes]))
            total = dot(star_rows[:, across], high)
            if exact:
                total += dot(star_rows[:, across], low)
            push_ref[:, lanes] += total
            pull_ref[:, across] += dot_t(body_rows[:, lanes], high)

    def all_pairs(first, last, start, stop, exact):
        if stop > start:
            width = block_of(stop - start, 512)
            sweep(start, stop, width, functools.partial(rectangle, first, last, width, exact))

    if before:
        all_pairs(n_held, n, 0, body_own, True)
        all_pairs(n_held, n, body_own, count_held, False)
        all_pairs(0, n, count_held, count, False)
    else:
        all_pairs(0, n, 0, body_own, True)
        all_pairs(0, n, body_own, count, False)
    total = mass_moment(push_ref[...], bodies[...] - middle)
    push[...] = total
    pull[...] = mass_moment(pull_ref[...], stars[...] - middle)[0:4]
    if before:
        push[:, :count_held] = held[7][...] + total[:, :count_held]
        pull[:, :n_held] = held[8][...] + pull[:, :n_held]


def kick(held, pieces, star_own, last):
    blocks = sum(piece.shape[0] for piece in pieces)
    body_own = pieces[0].shape[2] - star_own
    new = blocks * blocks
    if held:
        old = held[1].shape[1] // star_own
        new += 2 * old * blocks
        blocks += old
    n, count = blocks * star_own, blocks * body_own
    pairs = new * star_own * body_own
    shapes = [
        ((8, 128), f32),
        ((8, n), f32),
        ((8, count), f32),
        ((n, 48), bf16),
        ((48, count), bf16),
        ((16, n), bf16),
        ((16, count), bf16),
        ((8, count), f32),
        ((4, n), f32),
    ]
    scratch = []
    if last:
        scratch = [pltpu.VMEM(*shapes[k]) for k in (0, 3, 4, 5, 6)]
        shapes = [shapes[k] for k in (1, 2, 7, 8)]
    return pl.pallas_call(
        functools.partial(kick_kernel, star_own, bool(held), last, len(pieces)),
        out_shape=[jax.ShapeDtypeStruct(*shape) for shape in shapes],
        scratch_shapes=scratch + [pltpu.VMEM((16, n), f32), pltpu.VMEM((16, count), f32)],
        compiler_params=pltpu.CompilerParams(vmem_limit_bytes=vmem_limit),
        cost_estimate=pl.CostEstimate(flops=40 * pairs, bytes_accessed=0, transcendentals=pairs),
    )(*pieces, *held)


def first_kick(x, axis, star_own):
    pieces = gather_pieces(x, axis)
    held = kick([], pieces[:2], star_own, len(pieces) <= 2)
    for k, piece in enumerate(pieces[2:], 3):
        held = kick(held, [piece], star_own, k == len(pieces))
    return held


def drift_kernel(bodies_ref, push_ref, pos_out, vel_out, center_out, targets_out, rows_out):
    own = pos_out.shape[1]
    bodies = bodies_ref[...]
    row = row_of(bodies)
    moved = bodies + (step_time / 2.0) * rot(push_ref[...])
    moved = moved + jnp.where(row < 3, step_time * rot(moved), 0.0)
    pos_out[...] = moved[0:3, :own]
    vel_out[...] = moved[4:7, :own]
    middle = mean_of(moved)
    center_out[...] = jnp.broadcast_to(middle, center_out.shape)
    x = moved - middle
    targets_out[...] = distance_blocks(x, bridge_soft)[1].astype(bf16)
    rows_out[...] = mass_rows(x, bodies[3:4, :])


def drift(bodies, push, own):
    count = bodies.shape[1]
    return pl.pallas_call(
        drift_kernel,
        out_shape=[
            jax.ShapeDtypeStruct((3, own), f32),
            jax.ShapeDtypeStruct((3, own), f32),
            jax.ShapeDtypeStruct((8, 128), f32),
            jax.ShapeDtypeStruct((48, count), bf16),
            jax.ShapeDtypeStruct((16, count), bf16),
        ],
        compiler_params=pltpu.CompilerParams(vmem_limit_bytes=vmem_limit),
        cost_estimate=pl.CostEstimate(
            flops=2000 * count, bytes_accessed=200 * count, transcendentals=0
        ),
    )(bodies, push)


def push_kernel(stars_ref, center_ref, targets_ref, pos_ref, vel_ref, vel_out):
    own = vel_out.shape[1]
    stars = stars_ref[...]
    n = stars.shape[1]
    y = stars - center_ref[:, 0:1]
    source = distance_blocks(y, bridge_soft)[0].astype(bf16).T
    star_rows = mass_rows(y, stars[3:4, :])
    ti, tj = block_of(n, 1024), block_of(own, 256)
    for j in range(0, own, tj):
        total = jnp.zeros((16, tj), f32)
        for i in range(0, n, ti):
            high, low = split(weights(source[i : i + ti, :], targets_ref[:, j : j + tj]))
            total += dot(star_rows[:, i : i + ti], high) + dot(star_rows[:, i : i + ti], low)
        x = pos_ref[:, j : j + tj] - center_ref[0:3, 0:1]
        x = jnp.concatenate([x, jnp.zeros((5, tj), f32)], axis=0)
        push = mass_moment(total, x)[0:3]
        vel_out[:, j : j + tj] = vel_ref[:, j : j + tj] + (step_time / 2.0) * push


def second_push(stars, center, targets, pos, vel):
    pairs = stars.shape[1] * pos.shape[1]
    return pl.pallas_call(
        push_kernel,
        grid=(1,),
        in_specs=[
            pl.BlockSpec(stars.shape, lambda i: (0, 0)),
            pl.BlockSpec(center.shape, lambda i: (0, 0)),
            pl.BlockSpec((48, pos.shape[1]), lambda i: (0, 0)),
            pl.BlockSpec(pos.shape, lambda i: (0, 0)),
            pl.BlockSpec(vel.shape, lambda i: (0, 0)),
        ],
        out_specs=pl.BlockSpec(vel.shape, lambda i: (0, 0)),
        out_shape=jax.ShapeDtypeStruct(vel.shape, f32),
        compiler_params=pltpu.CompilerParams(vmem_limit_bytes=vmem_limit),
        cost_estimate=pl.CostEstimate(flops=40 * pairs, bytes_accessed=0, transcendentals=pairs),
    )(stars, center, targets, pos, vel)


def prepare_kernel(
    total_stars, total_bodies, species, pos, vel, mass, body_pos, body_vel, kind, out
):
    own = pos.shape[1]
    out[0, 0:3, :own] = pos[...]
    out[0, 3:4, :own] = mass[...] / total_stars
    out[0, 4:7, :own] = vel[...]
    out[0, 7:8, :] = jnp.zeros((1, out.shape[2]), f32)
    body_mass = jnp.zeros(kind.shape, f32)
    for k in range(species.shape[1]):
        body_mass = body_mass + jnp.where(kind[...] == k, species[:, k : k + 1], 0.0)
    out[0, 0:3, own:] = body_pos[...]
    out[0, 3:4, own:] = body_mass / total_bodies
    out[0, 4:7, own:] = body_vel[...]


def prepare(species, pos, vel, mass, body_pos, body_vel, kind, total_stars, total_bodies):
    return pl.pallas_call(
        functools.partial(prepare_kernel, total_stars, total_bodies),
        out_shape=jax.ShapeDtypeStruct((1, 8, pos.shape[1] + body_pos.shape[1]), f32),
    )(species[None], pos, vel, mass[None], body_pos, body_vel, kind[None])


def swap(x, axis, bits):
    count = lax.axis_size(axis)
    return lax.ppermute(x, axis, [(i, i ^ bits) for i in range(count)])


def radices(count):
    steps, bit = [], 1
    if count.bit_length() % 2 == 0:
        steps.append((1,))
        bit = 2
    while bit < count:
        steps.append((bit, 2 * bit, 3 * bit))
        bit *= 4
    return steps


def copy_kernel(ref, out):
    out[...] = ref[...]


def copy(x):
    return pl.pallas_call(
        copy_kernel,
        out_shape=jax.ShapeDtypeStruct(x.shape, x.dtype),
        compiler_params=pltpu.CompilerParams(vmem_limit_bytes=vmem_limit),
    )(x)


def gather_pieces(x, axis):
    pieces = [x]
    for step in radices(lax.axis_size(axis)):
        if len(pieces) > 1:
            pieces = [jnp.concatenate(pieces, axis=0)]
        swapped = [swap(pieces[0], axis, bits) for bits in step]
        if pieces[0] is x:
            pieces = [copy(x)]
        pieces = pieces + swapped
    return pieces


def sum_pieces(x, axis):
    pieces = [x]
    for step in radices(lax.axis_size(axis)):
        while len(pieces) > 1:
            pieces = [a + b for a, b in zip(pieces[::2], pieces[1::2])]
        pieces = pieces + [swap(pieces[0], axis, bits) for bits in step]
    return pieces


def local(
    cluster_pos, cluster_vel, cluster_mass, galaxy_pos, galaxy_vel, galaxy_kind, species_mass
):
    own = cluster_pos.shape[1]
    total_stars = own * lax.axis_size("sub")
    total_bodies = galaxy_pos.shape[1] * lax.axis_size("sub") * lax.axis_size("grp")
    block = prepare(
        species_mass,
        cluster_pos,
        cluster_vel,
        cluster_mass,
        galaxy_pos,
        galaxy_vel,
        galaxy_kind,
        total_stars,
        total_bodies,
    )
    stars, bodies, push, pull = first_kick(block, "sub", own)
    pulls = sum_pieces(pull, "grp")
    body_pos, body_vel, center, targets, body_rows = drift(bodies, push, galaxy_pos.shape[1])
    stars, end_pos, end_vel, pull = hermite(stars, center, targets, body_rows, pulls, own)
    pull = add_up(sum_pieces(pull, "grp"))
    body_vel = second_push(stars, center, targets, body_pos, body_vel)
    return end_pos, end_vel + (step_time / 2.0) * pull, body_pos, body_vel


def solution(mesh):
    return jax.shard_map(
        local,
        mesh=mesh,
        in_specs=(
            P(None, "sub"),
            P(None, "sub"),
            P("sub"),
            P(None, ("grp", "sub")),
            P(None, ("grp", "sub")),
            P(("grp", "sub")),
            P(),
        ),
        out_specs=(
            P(None, "sub"),
            P(None, "sub"),
            P(None, ("grp", "sub")),
            P(None, ("grp", "sub")),
        ),
        check_vma=False,
    )
```

```python
import functools

import jax
import jax.numpy as jnp
import numpy as np
from jax import lax
from jax.experimental import pallas as pl
from jax.experimental.pallas import tpu as pltpu
from jax.sharding import PartitionSpec as P

SUBSTEPS = 8

step_time = 0.5
bridge_soft = 0.01
cluster_soft = 0.0025
f32 = jnp.float32
bf16 = jnp.bfloat16
vmem_limit = 48 * 1024 * 1024


def parts(x, count):
    terms = []
    for _ in range(count):
        term = x.astype(bf16).astype(f32)
        terms.append(term)
        x = x - term
    return terms


def dot(a, b):
    return lax.dot_general(a, b, (((1,), (0,)), ((), ())), preferred_element_type=f32)


def dot_t(a, b):
    return lax.dot_general(a, b, (((1,), (1,)), ((), ())), preferred_element_type=f32)


def split(x):
    high = x.astype(bf16)
    return high, (x - high.astype(f32)).astype(bf16)


def block_of(count, most):
    size = most
    while count % size:
        size //= 2
    return size


def row_of(x):
    return lax.broadcasted_iota(jnp.int32, x.shape, 0)


def rot(x):
    return pltpu.roll(x, 4, 0)


def block(row, a, sa, b, sb):
    return jnp.where(row < 3, a, jnp.where(row == 3, sa, jnp.where(row < 7, b, sb)))


def constant_parts(value):
    terms = []
    for _ in range(3):
        term = float(np.asarray(value, bf16))
        terms.append(term)
        value -= term
    return terms


def fill(row, block, third, seventh):
    return jnp.where(row == 3, third, jnp.where(row == 7, seventh, block))


def grid_of(y):
    x = jnp.where(row_of(y) < 3, y, 0.0)
    grid = jnp.floor(x * 8.0 + 0.5) * 0.125
    rest = x - grid
    square = jnp.sum(grid * grid, axis=0, keepdims=True)
    return grid, rest, square, jnp.sum(rest * (grid + x), axis=0, keepdims=True)


def distance_rows(grid, rest, q, p, soften):
    row = row_of(grid)
    e = parts(rest, 3)
    f = [-2.0 * term for term in e]
    soft = constant_parts(soften)
    twice = -2.0 * grid
    rot_grid, rot_twice = rot(grid), rot(twice)
    rot_e, rot_f = rot(e[1]), rot(f[0])
    targets = [
        block(row, grid, q[0], jnp.where(row == 4, q[1], 1.0), 1.0),
        block(row, e[0], p[0], rot_e, p[1]),
        block(row, e[2], p[2], rot_grid, 1.0),
        block(row, grid, 1.0, rot_grid, 1.0),
        block(row, e[0], 1.0, rot_e, 1.0),
        e[0],
    ]
    last = jnp.where(row == 4, 1.0, jnp.where(row == 5, q[0], q[1]))
    sources = [
        block(row, twice, 1.0, last, soft[0]),
        block(row, twice, 1.0, rot_twice, 1.0),
        block(row, twice, 1.0, rot_f, p[0]),
        block(row, f[1], p[1], rot(f[2]), p[2]),
        block(row, f[0], soft[1], rot_f, soft[2]),
        f[1],
    ]
    return jnp.concatenate(sources, axis=0), jnp.concatenate(targets, axis=0)


def distance_blocks(y, soften):
    grid, rest, square, small = grid_of(y)
    return distance_rows(grid, rest, parts(square, 2), parts(small, 3), soften)


def phase_blocks(y):
    row = row_of(y)
    grid, rest, square, small = grid_of(y)
    product = jnp.sum(jnp.where(row < 3, y * rot(y), 0.0), axis=0, keepdims=True)
    scalars = parts(jnp.where(row == 0, square, jnp.where(row == 1, small, -product)), 3)
    q = [term[0:1] for term in scalars]
    p = [term[1:2] for term in scalars]
    c = [term[2:3] for term in scalars]
    source, target = distance_rows(grid, rest, q, p, cluster_soft)
    y1, y2, y3 = parts(y, 3)
    r1, r2, r3 = rot(y1), rot(y2), rot(y3)
    sources = [
        fill(row, y1, 1.0, c[0]),
        fill(row, y1, 1.0, c[1]),
        fill(row, y2, 1.0, c[2]),
        y2,
        y1,
        y3,
    ]
    targets = [
        fill(row, r1, c[0], 1.0),
        fill(row, r2, c[1], 1.0),
        fill(row, r1, c[2], 1.0),
        r2,
        r3,
        r1,
    ]
    sums = [
        fill(row, y1, 1.0, pltpu.roll(y3, 7, 0)),
        fill(row, y2, pltpu.roll(y3, 2, 0), pltpu.roll(y3, 5, 0)),
    ]
    return (
        jnp.concatenate([source] + sources, axis=0).astype(bf16),
        target.astype(bf16),
        jnp.concatenate(targets, axis=0).astype(bf16),
        jnp.concatenate(sums, axis=0).astype(bf16),
    )


def phase_moment(first, second, y):
    row = row_of(y)
    third = jnp.where(
        row == 0,
        pltpu.roll(first, 1, 0),
        jnp.where(
            row == 1, pltpu.roll(second, 6, 0), jnp.where(row == 2, pltpu.roll(second, 3, 0), 0.0)
        ),
    )
    return first + jnp.where(row == 3, 0.0, second) + third - y * first[3:4]


def mass_rows(y, mass):
    row = row_of(y)
    terms = parts(jnp.where(row < 3, mass * y, jnp.where(row == 3, mass, 0.0)), 3)
    return jnp.concatenate([terms[0] + rot(terms[1]), terms[2]], axis=0).astype(bf16)


def mass_moment(total, y):
    total = total[0:8] + rot(total[0:8]) + total[8:16]
    return jnp.where(row_of(y) < 3, total - y * total[3:4], 0.0)


def mean_of(y):
    mean = jnp.mean(y, axis=1, keepdims=True)
    return jnp.where(row_of(mean) < 3, mean, 0.0)


def weights(sources, targets):
    inverse = lax.rsqrt(dot(sources, targets))
    return inverse * inverse * inverse


def evaluate(y, mass_ref, refs):
    from_ref, to_ref, phase_ref, sum_ref = refs
    n = y.shape[1]
    row = row_of(y)
    y = fill(row, y, 0.0, 0.0)
    source, distance, closing, phase = phase_blocks(y)
    from_ref[...] = source.T
    phase_ref[...] = phase
    ti, tj = block_of(n, 1024), block_of(n, 128)
    for j in range(0, n, tj):
        to_ref[0:48, 2 * j : 2 * j + tj] = distance[:, j : j + tj]
        to_ref[48:96, 2 * j + tj : 2 * j + 2 * tj] = closing[:, j : j + tj]

    def weight_block(across, j):
        both = dot(from_ref[across, :], to_ref[:, pl.ds(2 * j, 2 * tj)])
        inverse = lax.rsqrt(both[:, :tj])
        square = inverse * inverse
        mass = jnp.concatenate([mass_ref[across, :]] * (tj // 128), axis=1)
        weight = square * (inverse * mass)
        radial = weight * square * both[:, tj:]
        return jnp.concatenate(
            [
                jnp.concatenate(split(weight), axis=0),
                jnp.concatenate(split(radial), axis=0),
            ],
            axis=1,
        )

    def sums(across, both):
        phase = phase_ref[:, across]
        return dot(jnp.concatenate([phase, phase], axis=1), both)

    def store(j, total):
        sum_ref[0:16, pl.ds(j, tj)] = total[:, :tj]
        sum_ref[16:32, pl.ds(j, tj)] = total[:, tj:]

    if n == ti:
        every = slice(0, n)
        waiting = None
        for j in range(0, n, tj):
            both = weight_block(every, j)
            if waiting is not None:
                store(j - tj, sums(every, waiting))
            waiting = both
        store(n - tj, sums(every, waiting))
    else:

        def one_block(k, carry):
            j = pl.multiple_of(k * tj, tj)
            total = jnp.zeros((16, 2 * tj), f32)
            for i in range(0, n, ti):
                across = slice(i, i + ti)
                total += sums(across, weight_block(across, j))
            store(j, total)
            return carry

        lax.fori_loop(0, n // tj, one_block, 0)
    direct = phase_moment(sum_ref[0:8, :], sum_ref[8:16, :], y)
    radial = phase_moment(sum_ref[16:24, :], sum_ref[24:32, :], y)
    return direct + jnp.where(row >= 4, 3.0 * rot(radial), 0.0)


def add_up(values):
    while len(values) > 1:
        values = [a + b for a, b in zip(values[::2], values[1::2])]
    return values[0]


def hermite_kernel(pull_count, stars_ref, center_ref, targets_ref, body_rows_ref, *refs):
    pulls, (stars_out, pos_out, vel_out, pull_out, mass_ref, *work) = (
        refs[:pull_count],
        refs[pull_count:],
    )
    own, count = pos_out.shape[1], targets_ref.shape[1]
    stars = stars_ref[...]
    n = stars.shape[1]
    row = row_of(stars)
    mass_ref[...] = jnp.broadcast_to(stars[3:4, :], (128, n)).T
    work[1][...] = jnp.zeros_like(work[1])
    pull = add_up([ref[...] for ref in pulls])
    y = jnp.where(row == 3, 0.0, stars)
    y = y + (step_time / 2.0) * jnp.concatenate([jnp.zeros_like(pull), pull], axis=0)
    frame = jnp.mean(y, axis=1, keepdims=True)
    y = y - frame
    h = step_time / SUBSTEPS
    pos_row, vel_row = row < 3, row >= 4
    guess_vel = jnp.where(pos_row, h, 0.0)
    guess_other = jnp.where(pos_row, h * h * h / 6.0, h)
    kick = jnp.where(vel_row, h / 2.0, 0.0)
    drift = jnp.where(pos_row, h / 2.0, 0.0)
    rates = evaluate(y, mass_ref, work)

    def substep(_, carry):
        y, rates = carry
        vel = rot(y)
        guess = y + guess_vel * vel + (h * h / 2.0) * rates + guess_other * rot(rates)
        fresh = evaluate(guess, mass_ref, work)
        z = y + (h * h / 12.0) * (rates - fresh) + kick * rot(rates + fresh)
        return z + drift * (vel + rot(z)), fresh

    y, _ = lax.fori_loop(0, SUBSTEPS, substep, (y, rates), unroll=True)
    frame = frame + jnp.where(row_of(frame) < 3, step_time * jnp.concatenate([frame[4:8], frame[0:4]], axis=0), 0.0)
    y = y + frame
    stars_out[...] = jnp.where(row == 3, stars, y)
    y = y[:, :own]
    pos_out[...] = y[0:3]
    vel_out[...] = y[4:7]
    y = y - center_ref[:, 0:1]
    source = distance_blocks(y, bridge_soft)[0].astype(bf16).T
    tj = block_of(count, 2048)
    total = jnp.zeros((16, own), f32)
    for j in range(0, count, tj):
        weight = weights(source, targets_ref[:, j : j + tj]).astype(bf16)
        total += dot_t(body_rows_ref[:, j : j + tj], weight)
    pull_out[...] = mass_moment(total, y)[0:3]


def hermite(stars, center, body_targets, body_rows, pulls, own):
    n = stars.shape[1]
    pairs = n * n * (SUBSTEPS + 1)
    return pl.pallas_call(
        functools.partial(hermite_kernel, len(pulls)),
        out_shape=[
            jax.ShapeDtypeStruct(stars.shape, f32),
            jax.ShapeDtypeStruct((3, own), f32),
            jax.ShapeDtypeStruct((3, own), f32),
            jax.ShapeDtypeStruct((3, own), f32),
        ],
        scratch_shapes=[
            pltpu.VMEM((n, 128), f32),
            pltpu.VMEM((n, 96), bf16),
            pltpu.VMEM((96, 2 * n), bf16),
            pltpu.VMEM((16, n), bf16),
            pltpu.VMEM((32, n), f32),
        ],
        compiler_params=pltpu.CompilerParams(vmem_limit_bytes=vmem_limit),
        cost_estimate=pl.CostEstimate(flops=80 * pairs, bytes_accessed=0, transcendentals=pairs),
    )(stars, center, body_targets, body_rows, *pulls)


def sweep(start, stop, step, body):
    if (stop - start) // step <= 8:
        for j in range(start, stop, step):
            body(j)
        return

    def one(k, carry):
        body(pl.multiple_of(start + k * step, step))
        return carry

    lax.fori_loop(0, (stop - start) // step, one, 0)


def kick_kernel(star_own, before, last, piece_count, *refs):
    pieces, refs = refs[:piece_count], refs[piece_count:]
    held, refs = (refs[:9], refs[9:]) if before else (None, refs)
    if last:
        stars, bodies, push, pull, center, source, target, star_rows, body_rows = refs[:9]
    else:
        center, stars, bodies, source, target, star_rows, body_rows, push, pull = refs[:9]
    pull_ref, push_ref = refs[9:]
    body_own = pieces[0].shape[2] - star_own
    n, count = stars.shape[1], bodies.shape[1]
    n_held = count_held = 0
    if before:
        n_held, count_held = held[1].shape[1], held[2].shape[1]
        center[...] = held[0][...]
        source[:n_held, :] = held[3][...]
        for old, ref in ((held[1], stars), (held[5], star_rows)):
            ref[:, :n_held] = old[...]
        for old, ref in ((held[2], bodies), (held[4], target), (held[6], body_rows)):
            ref[:, :count_held] = old[...]
    slot = n_held // star_own
    for piece in pieces:
        for k in range(piece.shape[0]):
            stars[:, slot * star_own : (slot + 1) * star_own] = piece[k, :, :star_own]
            bodies[:, slot * body_own : (slot + 1) * body_own] = piece[k, :, star_own:]
            slot += 1
    if not before:
        center[...] = jnp.broadcast_to(mean_of(stars[...]), center.shape)
    middle = center[:, 0:1]
    y = stars[:, n_held:] - middle
    source[n_held:, :] = distance_blocks(y, bridge_soft)[0].astype(bf16).T
    star_rows[:, n_held:] = mass_rows(y, stars[3:4, n_held:])
    x = bodies[:, count_held:] - middle
    target[:, count_held:] = distance_blocks(x, bridge_soft)[1].astype(bf16)
    body_rows[:, count_held:] = mass_rows(x, bodies[3:4, count_held:])
    pull_ref[...] = jnp.zeros_like(pull_ref)
    push_ref[...] = jnp.zeros_like(push_ref)
    tj = block_of(body_own, 256)

    def rectangle(first, last, width, exact, j):
        lanes = pl.ds(j, width)
        ti = block_of(last - first, 1024)
        for i in range(first, last, ti):
            across = slice(i, i + ti)
            high, low = split(weights(source[across, :], target[:, lanes]))
            total = dot(star_rows[:, across], high)
            if exact:
                total += dot(star_rows[:, across], low)
            push_ref[:, lanes] += total
            pull_ref[:, across] += dot_t(body_rows[:, lanes], high)

    def all_pairs(first, last, start, stop, exact):
        if stop > start:
            width = block_of(stop - start, 512)
            sweep(start, stop, width, functools.partial(rectangle, first, last, width, exact))

    if before:
        all_pairs(n_held, n, 0, body_own, True)
        all_pairs(n_held, n, body_own, count_held, False)
        all_pairs(0, n, count_held, count, False)
    else:
        all_pairs(0, n, 0, body_own, True)
        all_pairs(0, n, body_own, count, False)
    total = mass_moment(push_ref[...], bodies[...] - middle)
    push[...] = total
    pull[...] = mass_moment(pull_ref[...], stars[...] - middle)[0:4]
    if before:
        push[:, :count_held] = held[7][...] + total[:, :count_held]
        pull[:, :n_held] = held[8][...] + pull[:, :n_held]


def kick(held, pieces, star_own, last):
    blocks = sum(piece.shape[0] for piece in pieces)
    body_own = pieces[0].shape[2] - star_own
    new = blocks * blocks
    if held:
        old = held[1].shape[1] // star_own
        new += 2 * old * blocks
        blocks += old
    n, count = blocks * star_own, blocks * body_own
    pairs = new * star_own * body_own
    shapes = [
        ((8, 128), f32),
        ((8, n), f32),
        ((8, count), f32),
        ((n, 48), bf16),
        ((48, count), bf16),
        ((16, n), bf16),
        ((16, count), bf16),
        ((8, count), f32),
        ((4, n), f32),
    ]
    scratch = []
    if last:
        scratch = [pltpu.VMEM(*shapes[k]) for k in (0, 3, 4, 5, 6)]
        shapes = [shapes[k] for k in (1, 2, 7, 8)]
    return pl.pallas_call(
        functools.partial(kick_kernel, star_own, bool(held), last, len(pieces)),
        out_shape=[jax.ShapeDtypeStruct(*shape) for shape in shapes],
        scratch_shapes=scratch + [pltpu.VMEM((16, n), f32), pltpu.VMEM((16, count), f32)],
        compiler_params=pltpu.CompilerParams(vmem_limit_bytes=vmem_limit),
        cost_estimate=pl.CostEstimate(flops=40 * pairs, bytes_accessed=0, transcendentals=pairs),
    )(*pieces, *held)


def first_kick(x, axis, star_own):
    pieces = gather_pieces(x, axis)
    held = kick([], pieces[:2], star_own, len(pieces) <= 2)
    for k, piece in enumerate(pieces[2:], 3):
        held = kick(held, [piece], star_own, k == len(pieces))
    return held


def drift_kernel(bodies_ref, push_ref, pos_out, vel_out, center_out, targets_out, rows_out):
    own = pos_out.shape[1]
    bodies = bodies_ref[...]
    row = row_of(bodies)
    moved = bodies + (step_time / 2.0) * rot(push_ref[...])
    moved = moved + jnp.where(row < 3, step_time * rot(moved), 0.0)
    pos_out[...] = moved[0:3, :own]
    vel_out[...] = moved[4:7, :own]
    middle = mean_of(moved)
    center_out[...] = jnp.broadcast_to(middle, center_out.shape)
    x = moved - middle
    targets_out[...] = distance_blocks(x, bridge_soft)[1].astype(bf16)
    rows_out[...] = mass_rows(x, bodies[3:4, :])


def drift(bodies, push, own):
    count = bodies.shape[1]
    return pl.pallas_call(
        drift_kernel,
        out_shape=[
            jax.ShapeDtypeStruct((3, own), f32),
            jax.ShapeDtypeStruct((3, own), f32),
            jax.ShapeDtypeStruct((8, 128), f32),
            jax.ShapeDtypeStruct((48, count), bf16),
            jax.ShapeDtypeStruct((16, count), bf16),
        ],
        compiler_params=pltpu.CompilerParams(vmem_limit_bytes=vmem_limit),
        cost_estimate=pl.CostEstimate(
            flops=2000 * count, bytes_accessed=200 * count, transcendentals=0
        ),
    )(bodies, push)


def push_kernel(stars_ref, center_ref, targets_ref, pos_ref, vel_ref, vel_out):
    own = vel_out.shape[1]
    stars = stars_ref[...]
    n = stars.shape[1]
    y = stars - center_ref[:, 0:1]
    source = distance_blocks(y, bridge_soft)[0].astype(bf16).T
    star_rows = mass_rows(y, stars[3:4, :])
    ti, tj = block_of(n, 1024), block_of(own, 256)
    for j in range(0, own, tj):
        total = jnp.zeros((16, tj), f32)
        for i in range(0, n, ti):
            high, low = split(weights(source[i : i + ti, :], targets_ref[:, j : j + tj]))
            total += dot(star_rows[:, i : i + ti], high) + dot(star_rows[:, i : i + ti], low)
        x = pos_ref[:, j : j + tj] - center_ref[0:3, 0:1]
        x = jnp.concatenate([x, jnp.zeros((5, tj), f32)], axis=0)
        push = mass_moment(total, x)[0:3]
        vel_out[:, j : j + tj] = vel_ref[:, j : j + tj] + (step_time / 2.0) * push


def second_push(stars, center, targets, pos, vel):
    pairs = stars.shape[1] * pos.shape[1]
    return pl.pallas_call(
        push_kernel,
        grid=(1,),
        in_specs=[
            pl.BlockSpec(stars.shape, lambda i: (0, 0)),
            pl.BlockSpec(center.shape, lambda i: (0, 0)),
            pl.BlockSpec((48, pos.shape[1]), lambda i: (0, 0)),
            pl.BlockSpec(pos.shape, lambda i: (0, 0)),
            pl.BlockSpec(vel.shape, lambda i: (0, 0)),
        ],
        out_specs=pl.BlockSpec(vel.shape, lambda i: (0, 0)),
        out_shape=jax.ShapeDtypeStruct(vel.shape, f32),
        compiler_params=pltpu.CompilerParams(vmem_limit_bytes=vmem_limit),
        cost_estimate=pl.CostEstimate(flops=40 * pairs, bytes_accessed=0, transcendentals=pairs),
    )(stars, center, targets, pos, vel)


def prepare_kernel(
    total_stars, total_bodies, species, pos, vel, mass, body_pos, body_vel, kind, out
):
    own = pos.shape[1]
    out[0, 0:3, :own] = pos[...]
    out[0, 3:4, :own] = mass[...] / total_stars
    out[0, 4:7, :own] = vel[...]
    out[0, 7:8, :] = jnp.zeros((1, out.shape[2]), f32)
    body_mass = jnp.zeros(kind.shape, f32)
    for k in range(species.shape[1]):
        body_mass = body_mass + jnp.where(kind[...] == k, species[:, k : k + 1], 0.0)
    out[0, 0:3, own:] = body_pos[...]
    out[0, 3:4, own:] = body_mass / total_bodies
    out[0, 4:7, own:] = body_vel[...]


def prepare(species, pos, vel, mass, body_pos, body_vel, kind, total_stars, total_bodies):
    return pl.pallas_call(
        functools.partial(prepare_kernel, total_stars, total_bodies),
        out_shape=jax.ShapeDtypeStruct((1, 8, pos.shape[1] + body_pos.shape[1]), f32),
    )(species[None], pos, vel, mass[None], body_pos, body_vel, kind[None])


def swap(x, axis, bits):
    count = lax.axis_size(axis)
    return lax.ppermute(x, axis, [(i, i ^ bits) for i in range(count)])


def radices(count):
    steps, bit = [], 1
    if count.bit_length() % 2 == 0:
        steps.append((1,))
        bit = 2
    while bit < count:
        steps.append((bit, 2 * bit, 3 * bit) if bit == 1 else (2 * bit, bit, 3 * bit))
        bit *= 4
    return steps


def copy_kernel(ref, out):
    out[...] = ref[...]


def copy(x):
    return pl.pallas_call(
        copy_kernel,
        out_shape=jax.ShapeDtypeStruct(x.shape, x.dtype),
        compiler_params=pltpu.CompilerParams(vmem_limit_bytes=vmem_limit),
    )(x)


def gather_pieces(x, axis):
    pieces = [x]
    for step in radices(lax.axis_size(axis)):
        if len(pieces) > 1:
            pieces = [jnp.concatenate(pieces, axis=0)]
        swapped = [swap(pieces[0], axis, bits) for bits in step]
        if pieces[0] is x:
            pieces = [copy(x)]
        pieces = pieces + swapped
    return pieces


def sum_pieces(x, axis):
    pieces = [x]
    for step in radices(lax.axis_size(axis)):
        while len(pieces) > 1:
            pieces = [a + b for a, b in zip(pieces[::2], pieces[1::2])]
        pieces = pieces + [swap(pieces[0], axis, bits) for bits in step]
    return pieces


def local(
    cluster_pos, cluster_vel, cluster_mass, galaxy_pos, galaxy_vel, galaxy_kind, species_mass
):
    own = cluster_pos.shape[1]
    total_stars = own * lax.axis_size("sub")
    total_bodies = galaxy_pos.shape[1] * lax.axis_size("sub") * lax.axis_size("grp")
    block = prepare(
        species_mass,
        cluster_pos,
        cluster_vel,
        cluster_mass,
        galaxy_pos,
        galaxy_vel,
        galaxy_kind,
        total_stars,
        total_bodies,
    )
    stars, bodies, push, pull = first_kick(block, "sub", own)
    pulls = sum_pieces(pull, "grp")
    body_pos, body_vel, center, targets, body_rows = drift(bodies, push, galaxy_pos.shape[1])
    stars, end_pos, end_vel, pull = hermite(stars, center, targets, body_rows, pulls, own)
    pull = add_up(sum_pieces(pull, "grp"))
    body_vel = second_push(stars, center, targets, body_pos, body_vel)
    return end_pos, end_vel + (step_time / 2.0) * pull, body_pos, body_vel


def solution(mesh):
    return jax.shard_map(
        local,
        mesh=mesh,
        in_specs=(
            P(None, "sub"),
            P(None, "sub"),
            P("sub"),
            P(None, ("grp", "sub")),
            P(None, ("grp", "sub")),
            P(("grp", "sub")),
            P(),
        ),
        out_specs=(
            P(None, "sub"),
            P(None, "sub"),
            P(None, ("grp", "sub")),
            P(None, ("grp", "sub")),
        ),
        check_vma=False,
    )
```

```python
import functools

import jax
import jax.numpy as jnp
import numpy as np
from jax import lax
from jax.experimental import pallas as pl
from jax.experimental.pallas import tpu as pltpu
from jax.sharding import PartitionSpec as P

SUBSTEPS = 8

step_time = 0.5
bridge_soft = 0.01
cluster_soft = 0.0025
f32 = jnp.float32
bf16 = jnp.bfloat16
vmem_limit = 48 * 1024 * 1024


def parts(x, count):
    terms = []
    for _ in range(count):
        term = x.astype(bf16).astype(f32)
        terms.append(term)
        x = x - term
    return terms


def dot(a, b):
    return lax.dot_general(a, b, (((1,), (0,)), ((), ())), preferred_element_type=f32)


def dot_t(a, b):
    return lax.dot_general(a, b, (((1,), (1,)), ((), ())), preferred_element_type=f32)


def split(x):
    high = x.astype(bf16)
    return high, (x - high.astype(f32)).astype(bf16)


def block_of(count, most):
    size = most
    while count % size:
        size //= 2
    return size


def row_of(x):
    return lax.broadcasted_iota(jnp.int32, x.shape, 0)


def rot(x):
    return pltpu.roll(x, 4, 0)


def block(row, a, sa, b, sb):
    return jnp.where(row < 3, a, jnp.where(row == 3, sa, jnp.where(row < 7, b, sb)))


def constant_parts(value):
    terms = []
    for _ in range(3):
        term = float(np.asarray(value, bf16))
        terms.append(term)
        value -= term
    return terms


def fill(row, block, third, seventh):
    return jnp.where(row == 3, third, jnp.where(row == 7, seventh, block))


def grid_of(y):
    x = jnp.where(row_of(y) < 3, y, 0.0)
    grid = jnp.floor(x * 8.0 + 0.5) * 0.125
    rest = x - grid
    square = jnp.sum(grid * grid, axis=0, keepdims=True)
    return grid, rest, square, jnp.sum(rest * (grid + x), axis=0, keepdims=True)


def distance_rows(grid, rest, q, p, soften):
    row = row_of(grid)
    e = parts(rest, 3)
    f = [-2.0 * term for term in e]
    soft = constant_parts(soften)
    twice = -2.0 * grid
    rot_grid, rot_twice = rot(grid), rot(twice)
    rot_e, rot_f = rot(e[1]), rot(f[0])
    targets = [
        block(row, grid, q[0], jnp.where(row == 4, q[1], 1.0), 1.0),
        block(row, e[0], p[0], rot_e, p[1]),
        block(row, e[2], p[2], rot_grid, 1.0),
        block(row, grid, 1.0, rot_grid, 1.0),
        block(row, e[0], 1.0, rot_e, 1.0),
        e[0],
    ]
    last = jnp.where(row == 4, 1.0, jnp.where(row == 5, q[0], q[1]))
    sources = [
        block(row, twice, 1.0, last, soft[0]),
        block(row, twice, 1.0, rot_twice, 1.0),
        block(row, twice, 1.0, rot_f, p[0]),
        block(row, f[1], p[1], rot(f[2]), p[2]),
        block(row, f[0], soft[1], rot_f, soft[2]),
        f[1],
    ]
    return jnp.concatenate(sources, axis=0), jnp.concatenate(targets, axis=0)


def distance_blocks(y, soften):
    grid, rest, square, small = grid_of(y)
    return distance_rows(grid, rest, parts(square, 2), parts(small, 3), soften)


def phase_blocks(y):
    row = row_of(y)
    grid, rest, square, small = grid_of(y)
    product = jnp.sum(jnp.where(row < 3, y * rot(y), 0.0), axis=0, keepdims=True)
    scalars = parts(jnp.where(row == 0, square, jnp.where(row == 1, small, -product)), 3)
    q = [term[0:1] for term in scalars]
    p = [term[1:2] for term in scalars]
    c = [term[2:3] for term in scalars]
    source, target = distance_rows(grid, rest, q, p, cluster_soft)
    y1, y2, y3 = parts(y, 3)
    r1, r2, r3 = rot(y1), rot(y2), rot(y3)
    sources = [
        fill(row, y1, 1.0, c[0]),
        fill(row, y1, 1.0, c[1]),
        fill(row, y2, 1.0, c[2]),
        y2,
        y1,
        y3,
    ]
    targets = [
        fill(row, r1, c[0], 1.0),
        fill(row, r2, c[1], 1.0),
        fill(row, r1, c[2], 1.0),
        r2,
        r3,
        r1,
    ]
    sums = [
        fill(row, y1, 1.0, pltpu.roll(y3, 7, 0)),
        fill(row, y2, pltpu.roll(y3, 2, 0), pltpu.roll(y3, 5, 0)),
    ]
    return (
        jnp.concatenate([source] + sources, axis=0).astype(bf16),
        target.astype(bf16),
        jnp.concatenate(targets, axis=0).astype(bf16),
        jnp.concatenate(sums, axis=0).astype(bf16),
    )


def phase_moment(first, second, y):
    row = row_of(y)
    third = jnp.where(
        row == 0,
        pltpu.roll(first, 1, 0),
        jnp.where(
            row == 1, pltpu.roll(second, 6, 0), jnp.where(row == 2, pltpu.roll(second, 3, 0), 0.0)
        ),
    )
    return first + jnp.where(row == 3, 0.0, second) + third - y * first[3:4]


def mass_rows(y, mass):
    row = row_of(y)
    terms = parts(jnp.where(row < 3, mass * y, jnp.where(row == 3, mass, 0.0)), 3)
    return jnp.concatenate([terms[0] + rot(terms[1]), terms[2]], axis=0).astype(bf16)


def mass_moment(total, y):
    total = total[0:8] + rot(total[0:8]) + total[8:16]
    return jnp.where(row_of(y) < 3, total - y * total[3:4], 0.0)


def mean_of(y):
    mean = jnp.mean(y, axis=1, keepdims=True)
    return jnp.where(row_of(mean) < 3, mean, 0.0)


def weights(sources, targets):
    inverse = lax.rsqrt(dot(sources, targets))
    return inverse * inverse * inverse


def evaluate(y, mass_ref, refs):
    from_ref, to_ref, phase_ref, sum_ref = refs
    n = y.shape[1]
    row = row_of(y)
    y = fill(row, y, 0.0, 0.0)
    source, distance, closing, phase = phase_blocks(y)
    from_ref[...] = source.T
    phase_ref[...] = phase
    ti, tj = block_of(n, 1024), block_of(n, 128)
    for j in range(0, n, tj):
        to_ref[0:48, 2 * j : 2 * j + tj] = distance[:, j : j + tj]
        to_ref[48:96, 2 * j + tj : 2 * j + 2 * tj] = closing[:, j : j + tj]

    def weight_block(across, j):
        both = dot(from_ref[across, :], to_ref[:, pl.ds(2 * j, 2 * tj)])
        inverse = lax.rsqrt(both[:, :tj])
        square = inverse * inverse
        mass = jnp.concatenate([mass_ref[across, :]] * (tj // 128), axis=1)
        weight = square * (inverse * mass)
        radial = weight * square * both[:, tj:]
        return jnp.concatenate(
            [
                jnp.concatenate(split(weight), axis=0),
                jnp.concatenate(split(radial), axis=0),
            ],
            axis=1,
        )

    def sums(across, both):
        phase = phase_ref[:, across]
        return dot(jnp.concatenate([phase, phase], axis=1), both)

    def store(j, total):
        sum_ref[0:16, pl.ds(j, tj)] = total[:, :tj]
        sum_ref[16:32, pl.ds(j, tj)] = total[:, tj:]

    if n == ti:
        every = slice(0, n)
        waiting = None
        for j in range(0, n, tj):
            both = weight_block(every, j)
            if waiting is not None:
                store(j - tj, sums(every, waiting))
            waiting = both
        store(n - tj, sums(every, waiting))
    else:

        def one_block(k, carry):
            j = pl.multiple_of(k * tj, tj)
            total = jnp.zeros((16, 2 * tj), f32)
            for i in range(0, n, ti):
                across = slice(i, i + ti)
                total += sums(across, weight_block(across, j))
            store(j, total)
            return carry

        lax.fori_loop(0, n // tj, one_block, 0)
    direct = phase_moment(sum_ref[0:8, :], sum_ref[8:16, :], y)
    radial = phase_moment(sum_ref[16:24, :], sum_ref[24:32, :], y)
    return direct + jnp.where(row >= 4, 3.0 * rot(radial), 0.0)


def add_up(values):
    while len(values) > 1:
        values = [a + b for a, b in zip(values[::2], values[1::2])]
    return values[0]


def hermite_kernel(pull_count, stars_ref, center_ref, targets_ref, body_rows_ref, *refs):
    pulls, (stars_out, pos_out, vel_out, pull_out, mass_ref, *work) = (
        refs[:pull_count],
        refs[pull_count:],
    )
    own, count = pos_out.shape[1], targets_ref.shape[1]
    stars = stars_ref[...]
    n = stars.shape[1]
    row = row_of(stars)
    mass_ref[...] = jnp.broadcast_to(stars[3:4, :], (128, n)).T
    work[1][...] = jnp.zeros_like(work[1])
    pull = add_up([ref[...] for ref in pulls])
    y = jnp.where(row == 3, 0.0, stars)
    y = y + (step_time / 2.0) * jnp.concatenate([jnp.zeros_like(pull), pull], axis=0)
    frame = jnp.mean(y, axis=1, keepdims=True)
    y = y - frame
    h = step_time / SUBSTEPS
    pos_row, vel_row = row < 3, row >= 4
    guess_vel = jnp.where(pos_row, h, 0.0)
    guess_other = jnp.where(pos_row, h * h * h / 6.0, h)
    kick = jnp.where(vel_row, h / 2.0, 0.0)
    drift = jnp.where(pos_row, h / 2.0, 0.0)
    rates = evaluate(y, mass_ref, work)

    def substep(_, carry):
        y, rates = carry
        vel = rot(y)
        guess = y + guess_vel * vel + (h * h / 2.0) * rates + guess_other * rot(rates)
        fresh = evaluate(guess, mass_ref, work)
        z = y + (h * h / 12.0) * (rates - fresh) + kick * rot(rates + fresh)
        return z + drift * (vel + rot(z)), fresh

    y, _ = lax.fori_loop(0, SUBSTEPS, substep, (y, rates), unroll=True)
    frame = frame + jnp.where(row_of(frame) < 3, step_time * jnp.concatenate([frame[4:8], frame[0:4]], axis=0), 0.0)
    y = y + frame
    stars_out[...] = jnp.where(row == 3, stars, y)
    y = y[:, :own]
    pos_out[...] = y[0:3]
    vel_out[...] = y[4:7]
    y = y - center_ref[:, 0:1]
    source = distance_blocks(y, bridge_soft)[0].astype(bf16).T
    tj = block_of(count, 2048)
    total = jnp.zeros((16, own), f32)
    for j in range(0, count, tj):
        terms = split(weights(source, targets_ref[:, j : j + tj]))
        moments = body_rows_ref[:, j : j + tj]
        total += dot_t(
            jnp.concatenate([moments, moments], axis=1), jnp.concatenate(terms, axis=1)
        )
    pull_out[...] = mass_moment(total, y)[0:3]


def hermite(stars, center, body_targets, body_rows, pulls, own):
    n = stars.shape[1]
    pairs = n * n * (SUBSTEPS + 1)
    return pl.pallas_call(
        functools.partial(hermite_kernel, len(pulls)),
        out_shape=[
            jax.ShapeDtypeStruct(stars.shape, f32),
            jax.ShapeDtypeStruct((3, own), f32),
            jax.ShapeDtypeStruct((3, own), f32),
            jax.ShapeDtypeStruct((3, own), f32),
        ],
        scratch_shapes=[
            pltpu.VMEM((n, 128), f32),
            pltpu.VMEM((n, 96), bf16),
            pltpu.VMEM((96, 2 * n), bf16),
            pltpu.VMEM((16, n), bf16),
            pltpu.VMEM((32, n), f32),
        ],
        compiler_params=pltpu.CompilerParams(vmem_limit_bytes=vmem_limit),
        cost_estimate=pl.CostEstimate(flops=80 * pairs, bytes_accessed=0, transcendentals=pairs),
    )(stars, center, body_targets, body_rows, *pulls)


def sweep(start, stop, step, body):
    if (stop - start) // step <= 8:
        for j in range(start, stop, step):
            body(j)
        return

    def one(k, carry):
        body(pl.multiple_of(start + k * step, step))
        return carry

    lax.fori_loop(0, (stop - start) // step, one, 0)


def kick_kernel(star_own, before, last, piece_count, *refs):
    pieces, refs = refs[:piece_count], refs[piece_count:]
    held, refs = (refs[:9], refs[9:]) if before else (None, refs)
    if last:
        stars, bodies, push, pull, center, source, target, star_rows, body_rows = refs[:9]
    else:
        center, stars, bodies, source, target, star_rows, body_rows, push, pull = refs[:9]
    pull_ref, push_ref = refs[9:]
    body_own = pieces[0].shape[2] - star_own
    n, count = stars.shape[1], bodies.shape[1]
    n_held = count_held = 0
    if before:
        n_held, count_held = held[1].shape[1], held[2].shape[1]
        center[...] = held[0][...]
        source[:n_held, :] = held[3][...]
        for old, ref in ((held[1], stars), (held[5], star_rows)):
            ref[:, :n_held] = old[...]
        for old, ref in ((held[2], bodies), (held[4], target), (held[6], body_rows)):
            ref[:, :count_held] = old[...]
    slot = n_held // star_own
    for piece in pieces:
        for k in range(piece.shape[0]):
            stars[:, slot * star_own : (slot + 1) * star_own] = piece[k, :, :star_own]
            bodies[:, slot * body_own : (slot + 1) * body_own] = piece[k, :, star_own:]
            slot += 1
    if not before:
        center[...] = jnp.broadcast_to(mean_of(stars[...]), center.shape)
    middle = center[:, 0:1]
    y = stars[:, n_held:] - middle
    source[n_held:, :] = distance_blocks(y, bridge_soft)[0].astype(bf16).T
    star_rows[:, n_held:] = mass_rows(y, stars[3:4, n_held:])
    x = bodies[:, count_held:] - middle
    target[:, count_held:] = distance_blocks(x, bridge_soft)[1].astype(bf16)
    body_rows[:, count_held:] = mass_rows(x, bodies[3:4, count_held:])
    pull_ref[...] = jnp.zeros_like(pull_ref)
    push_ref[...] = jnp.zeros_like(push_ref)
    def rectangle(first, last, width, j):
        lanes = pl.ds(j, width)
        ti = block_of(last - first, 1024)
        moments = body_rows[:, lanes]
        for i in range(first, last, ti):
            across = slice(i, i + ti)
            terms = split(weights(source[across, :], target[:, lanes]))
            sums = star_rows[:, across]
            push_ref[:, lanes] += dot(
                jnp.concatenate([sums, sums], axis=1), jnp.concatenate(terms, axis=0)
            )
            pull_ref[:, across] += dot_t(
                jnp.concatenate([moments, moments], axis=1), jnp.concatenate(terms, axis=1)
            )

    def all_pairs(first, last, start, stop):
        width = block_of(stop - start, 512)
        sweep(start, stop, width, functools.partial(rectangle, first, last, width))

    if before:
        all_pairs(n_held, n, 0, count_held)
    all_pairs(0, n, count_held, count)
    total = mass_moment(push_ref[...], bodies[...] - middle)
    push[...] = total
    pull[...] = mass_moment(pull_ref[...], stars[...] - middle)[0:4]
    if before:
        push[:, :count_held] = held[7][...] + total[:, :count_held]
        pull[:, :n_held] = held[8][...] + pull[:, :n_held]


def kick(held, pieces, star_own, last):
    blocks = sum(piece.shape[0] for piece in pieces)
    body_own = pieces[0].shape[2] - star_own
    new = blocks * blocks
    if held:
        old = held[1].shape[1] // star_own
        new += 2 * old * blocks
        blocks += old
    n, count = blocks * star_own, blocks * body_own
    pairs = new * star_own * body_own
    shapes = [
        ((8, 128), f32),
        ((8, n), f32),
        ((8, count), f32),
        ((n, 48), bf16),
        ((48, count), bf16),
        ((16, n), bf16),
        ((16, count), bf16),
        ((8, count), f32),
        ((4, n), f32),
    ]
    scratch = []
    if last:
        scratch = [pltpu.VMEM(*shapes[k]) for k in (0, 3, 4, 5, 6)]
        shapes = [shapes[k] for k in (1, 2, 7, 8)]
    return pl.pallas_call(
        functools.partial(kick_kernel, star_own, bool(held), last, len(pieces)),
        out_shape=[jax.ShapeDtypeStruct(*shape) for shape in shapes],
        scratch_shapes=scratch + [pltpu.VMEM((16, n), f32), pltpu.VMEM((16, count), f32)],
        compiler_params=pltpu.CompilerParams(vmem_limit_bytes=vmem_limit),
        cost_estimate=pl.CostEstimate(flops=40 * pairs, bytes_accessed=0, transcendentals=pairs),
    )(*pieces, *held)


def first_kick(x, axis, star_own):
    pieces = gather_pieces(x, axis)
    held = kick([], pieces[:2], star_own, len(pieces) <= 2)
    for k, piece in enumerate(pieces[2:], 3):
        held = kick(held, [piece], star_own, k == len(pieces))
    return held


def drift_kernel(bodies_ref, push_ref, pos_out, vel_out, center_out, targets_out, rows_out):
    own = pos_out.shape[1]
    bodies = bodies_ref[...]
    row = row_of(bodies)
    moved = bodies + (step_time / 2.0) * rot(push_ref[...])
    moved = moved + jnp.where(row < 3, step_time * rot(moved), 0.0)
    pos_out[...] = moved[0:3, :own]
    vel_out[...] = moved[4:7, :own]
    middle = mean_of(moved)
    center_out[...] = jnp.broadcast_to(middle, center_out.shape)
    x = moved - middle
    targets_out[...] = distance_blocks(x, bridge_soft)[1].astype(bf16)
    rows_out[...] = mass_rows(x, bodies[3:4, :])


def drift(bodies, push, own):
    count = bodies.shape[1]
    return pl.pallas_call(
        drift_kernel,
        out_shape=[
            jax.ShapeDtypeStruct((3, own), f32),
            jax.ShapeDtypeStruct((3, own), f32),
            jax.ShapeDtypeStruct((8, 128), f32),
            jax.ShapeDtypeStruct((48, count), bf16),
            jax.ShapeDtypeStruct((16, count), bf16),
        ],
        compiler_params=pltpu.CompilerParams(vmem_limit_bytes=vmem_limit),
        cost_estimate=pl.CostEstimate(
            flops=2000 * count, bytes_accessed=200 * count, transcendentals=0
        ),
    )(bodies, push)


def push_kernel(stars_ref, center_ref, targets_ref, pos_ref, vel_ref, vel_out):
    own = vel_out.shape[1]
    stars = stars_ref[...]
    n = stars.shape[1]
    y = stars - center_ref[:, 0:1]
    source = distance_blocks(y, bridge_soft)[0].astype(bf16).T
    star_rows = mass_rows(y, stars[3:4, :])
    ti, tj = block_of(n, 1024), block_of(own, 256)
    for j in range(0, own, tj):
        total = jnp.zeros((16, tj), f32)
        for i in range(0, n, ti):
            high, low = split(weights(source[i : i + ti, :], targets_ref[:, j : j + tj]))
            total += dot(star_rows[:, i : i + ti], high) + dot(star_rows[:, i : i + ti], low)
        x = pos_ref[:, j : j + tj] - center_ref[0:3, 0:1]
        x = jnp.concatenate([x, jnp.zeros((5, tj), f32)], axis=0)
        push = mass_moment(total, x)[0:3]
        vel_out[:, j : j + tj] = vel_ref[:, j : j + tj] + (step_time / 2.0) * push


def second_push(stars, center, targets, pos, vel):
    pairs = stars.shape[1] * pos.shape[1]
    return pl.pallas_call(
        push_kernel,
        grid=(1,),
        in_specs=[
            pl.BlockSpec(stars.shape, lambda i: (0, 0)),
            pl.BlockSpec(center.shape, lambda i: (0, 0)),
            pl.BlockSpec((48, pos.shape[1]), lambda i: (0, 0)),
            pl.BlockSpec(pos.shape, lambda i: (0, 0)),
            pl.BlockSpec(vel.shape, lambda i: (0, 0)),
        ],
        out_specs=pl.BlockSpec(vel.shape, lambda i: (0, 0)),
        out_shape=jax.ShapeDtypeStruct(vel.shape, f32),
        compiler_params=pltpu.CompilerParams(vmem_limit_bytes=vmem_limit),
        cost_estimate=pl.CostEstimate(flops=40 * pairs, bytes_accessed=0, transcendentals=pairs),
    )(stars, center, targets, pos, vel)


def prepare_kernel(
    total_stars, total_bodies, species, pos, vel, mass, body_pos, body_vel, kind, out
):
    own = pos.shape[1]
    out[0, 0:3, :own] = pos[...]
    out[0, 3:4, :own] = mass[...] / total_stars
    out[0, 4:7, :own] = vel[...]
    out[0, 7:8, :] = jnp.zeros((1, out.shape[2]), f32)
    body_mass = jnp.zeros(kind.shape, f32)
    for k in range(species.shape[1]):
        body_mass = body_mass + jnp.where(kind[...] == k, species[:, k : k + 1], 0.0)
    out[0, 0:3, own:] = body_pos[...]
    out[0, 3:4, own:] = body_mass / total_bodies
    out[0, 4:7, own:] = body_vel[...]


def prepare(species, pos, vel, mass, body_pos, body_vel, kind, total_stars, total_bodies):
    return pl.pallas_call(
        functools.partial(prepare_kernel, total_stars, total_bodies),
        out_shape=jax.ShapeDtypeStruct((1, 8, pos.shape[1] + body_pos.shape[1]), f32),
    )(species[None], pos, vel, mass[None], body_pos, body_vel, kind[None])


def swap(x, axis, bits):
    count = lax.axis_size(axis)
    return lax.ppermute(x, axis, [(i, i ^ bits) for i in range(count)])


def radices(count):
    steps, bit = [], 1
    if count.bit_length() % 2 == 0:
        steps.append((1,))
        bit = 2
    while bit < count:
        steps.append((bit, 2 * bit, 3 * bit) if bit == 1 else (2 * bit, bit, 3 * bit))
        bit *= 4
    return steps


def copy_kernel(ref, out):
    out[...] = ref[...]


def copy(x):
    return pl.pallas_call(
        copy_kernel,
        out_shape=jax.ShapeDtypeStruct(x.shape, x.dtype),
        compiler_params=pltpu.CompilerParams(vmem_limit_bytes=vmem_limit),
    )(x)


def gather_pieces(x, axis):
    pieces = [x]
    for step in radices(lax.axis_size(axis)):
        if len(pieces) > 1:
            pieces = [jnp.concatenate(pieces, axis=0)]
        swapped = [swap(pieces[0], axis, bits) for bits in step]
        if pieces[0] is x:
            pieces = [copy(x)]
        pieces = pieces + swapped
    return pieces


def sum_pieces(x, axis):
    pieces = [x]
    for step in radices(lax.axis_size(axis)):
        while len(pieces) > 1:
            pieces = [a + b for a, b in zip(pieces[::2], pieces[1::2])]
        pieces = pieces + [swap(pieces[0], axis, bits) for bits in step]
    return pieces


def local(
    cluster_pos, cluster_vel, cluster_mass, galaxy_pos, galaxy_vel, galaxy_kind, species_mass
):
    own = cluster_pos.shape[1]
    total_stars = own * lax.axis_size("sub")
    total_bodies = galaxy_pos.shape[1] * lax.axis_size("sub") * lax.axis_size("grp")
    block = prepare(
        species_mass,
        cluster_pos,
        cluster_vel,
        cluster_mass,
        galaxy_pos,
        galaxy_vel,
        galaxy_kind,
        total_stars,
        total_bodies,
    )
    stars, bodies, push, pull = first_kick(block, "sub", own)
    pulls = sum_pieces(pull, "grp")
    body_pos, body_vel, center, targets, body_rows = drift(bodies, push, galaxy_pos.shape[1])
    stars, end_pos, end_vel, pull = hermite(stars, center, targets, body_rows, pulls, own)
    pull = add_up(sum_pieces(pull, "grp"))
    body_vel = second_push(stars, center, targets, body_pos, body_vel)
    return end_pos, end_vel + (step_time / 2.0) * pull, body_pos, body_vel


def solution(mesh):
    return jax.shard_map(
        local,
        mesh=mesh,
        in_specs=(
            P(None, "sub"),
            P(None, "sub"),
            P("sub"),
            P(None, ("grp", "sub")),
            P(None, ("grp", "sub")),
            P(("grp", "sub")),
            P(),
        ),
        out_specs=(
            P(None, "sub"),
            P(None, "sub"),
            P(None, ("grp", "sub")),
            P(None, ("grp", "sub")),
        ),
        check_vma=False,
    )
```
